512 devices in a mesh: tmpl: 32 (over z, y_lo), sta: 16 (over y_hi, x, core).
Axes of the slice: x: 4, y: 8 (y_hi: 2, y_lo: 4; y = y_hi * 4 + y_lo), z: 8, core: 2. Of those that a mesh axis runs over, the one named last changes fastest.
Arguments:
- waveform: bfloat16 [1200, 5120], P('sta', 'tmpl'), may hold values from -40 to 40
- templates: bfloat16 [1024, 30, 400], P('tmpl'), may hold values from -5 to 5
- channel: int32 [1024, 30], P('tmpl'), may hold values from 0 to 1199, as said below
- moveout: int32 [1024, 30], P('tmpl'), may hold values from 0 to 399
Outputs:
- detection: float32 [1024, 4096], P('tmpl', 'sta')
The draws below stay inside these ranges and needn't reach their ends.
Inputs may be any that keep to these rules, and one draw needn't show every extreme that they name: `channel`: each template lists 30 distinct channels, the three components 3 q, 3 q + 1, 3 q + 2 of 10 stations q, in any slot order. Call the channels c with equal c // 75 a station group. A template's channels lie in two station groups g and (g + 1) modulo the number of groups, 15 in each. Among the 32 templates of one aligned block of rows, at most 150 entries fall into one station group, and exactly 150 into some group.
All inputs are finite; a program needn't handle non-finite values.
Results may differ from the reference program's by a relative error of at most 0.0029.
Values may be sent and summed in bfloat16 or wider, within the bound.
A program may use at most 64 MiB of HBM per device.

```python
import math
import jax
import jax.numpy as jnp
from jax import lax

CHANNELS = 1200
TEMPLATE_CHANS = 30
TEMPLATE_LENGTH = 400
BLOCK_SAMPLES = 128
STAT_SAMPLES = 4096
TPL_DEV = 32
FRAME_BLOCKS = 5
DATA = 5120
TEMPLATE_TOTAL = 1024
GROUP_STATIONS = 25
HOT = 8


def draw_waveform(key, part):
    key = jax.random.fold_in(key, 3)
    key_noise, key_level = jax.random.split(key)
    complete_shape = (CHANNELS, DATA)
    coarse_shape = (CHANNELS, DATA // 64)
    noise = jnp.clip(jax.random.normal(key_noise, complete_shape, jnp.float32), -4.0, 4.0)
    envelope = jnp.exp(jax.random.uniform(key_level, coarse_shape, jnp.float32, 0.0, math.log(10.0)))
    return (noise * jnp.repeat(envelope, 64, axis=1)).astype(jnp.bfloat16)


def draw_templates(key, part):
    key = jax.random.fold_in(key, 5)
    key_noise, key_amplitude_scale = jax.random.split(key)
    complete_shape = (TEMPLATE_TOTAL, TEMPLATE_CHANS, TEMPLATE_LENGTH)
    noise = jnp.clip(jax.random.normal(key_noise, complete_shape, jnp.float32), -5.0, 5.0)
    scale_values = jnp.exp(jax.random.uniform(key_amplitude_scale, (TEMPLATE_TOTAL, TEMPLATE_CHANS, 1), jnp.float32, math.log(0.1), 0.0))
    return (noise * scale_values).astype(jnp.bfloat16)


def draw_channel(key, part):
    key = jax.random.fold_in(key, 7)
    every_key = jax.random.split(key, 5)
    group_total = CHANNELS // (3 * GROUP_STATIONS)
    block_total = TEMPLATE_TOTAL // TPL_DEV
    busy_group = jax.random.randint(every_key[0], (block_total, 1), 0, group_total)
    ranking = jax.vmap(lambda single_key: jax.random.permutation(single_key, TPL_DEV))(jax.random.split(every_key[1], block_total))
    spread = (busy_group + 1 + jnp.maximum(ranking - HOT, 0) % (group_total - 1)) % group_total
    home_group = jnp.where(ranking < HOT, busy_group, spread).reshape(TEMPLATE_TOTAL)
    choose_home_group = jax.vmap(lambda single_key: jax.random.permutation(single_key, GROUP_STATIONS))(jax.random.split(every_key[2], TEMPLATE_TOTAL))[:, :TEMPLATE_CHANS // 6]
    choose_following = jax.vmap(lambda single_key: jax.random.permutation(single_key, GROUP_STATIONS))(jax.random.split(every_key[3], TEMPLATE_TOTAL))[:, :TEMPLATE_CHANS // 6]
    next_group = (home_group + 1) % group_total
    station_list = jnp.concatenate([home_group[:, None] * GROUP_STATIONS + choose_home_group, next_group[:, None] * GROUP_STATIONS + choose_following], axis=1)
    every_channel = (station_list[:, :, None] * 3 + jnp.arange(3, dtype=jnp.int32)[None, None, :]).reshape(TEMPLATE_TOTAL, TEMPLATE_CHANS)
    channel_slot_order = jax.vmap(lambda single_key: jax.random.permutation(single_key, TEMPLATE_CHANS))(jax.random.split(every_key[4], TEMPLATE_TOTAL))
    return jnp.take_along_axis(every_channel, channel_slot_order, axis=1).astype(jnp.int32)


def with_ends(array, stream_key, smallest, high):
    extent = array.shape
    place = [jax.random.randint(jax.random.fold_in(stream_key, axis), (), 0, extent[axis]) for axis in range(len(extent))]
    array = array.at[tuple(place)].set(smallest)
    longest = extent.index(max(extent))
    place[longest] = (place[longest] + 1) % extent[longest]
    return array.at[tuple(place)].set(high)


def setup_inputs(seed: int = 0) -> dict:
    arg_keys = jax.random.split(jax.random.key(seed), 5)
    return {
        "waveform": draw_waveform(jax.random.fold_in(arg_keys[4], 71), 0),
        "templates": draw_templates(jax.random.fold_in(arg_keys[4], 71), 0),
        "channel": draw_channel(jax.random.fold_in(arg_keys[4], 71), 0),
        "moveout": with_ends(jax.random.randint(arg_keys[3], (TEMPLATE_TOTAL, TEMPLATE_CHANS), 0, TEMPLATE_LENGTH), jax.random.fold_in(arg_keys[3], 1), 0, TEMPLATE_LENGTH - 1).astype(jnp.int32),
    }


def sliding_levels(waveform):
    squares = jnp.square(waveform.astype(jnp.float32))
    running = jnp.concatenate([jnp.zeros((squares.shape[0], 1), jnp.float32), jnp.cumsum(squares, axis=1)], axis=1)
    span_len = STAT_SAMPLES + TEMPLATE_LENGTH
    window_sum = running[:, TEMPLATE_LENGTH:TEMPLATE_LENGTH + span_len] - running[:, :span_len]
    return 1.0 / jnp.sqrt(window_sum / TEMPLATE_LENGTH + 1e-05)

def band_matrix(unit_rows):
    pair_count = unit_rows.shape[0]
    frame_len = BLOCK_SAMPLES * FRAME_BLOCKS
    padded = jnp.concatenate([jnp.zeros((pair_count, BLOCK_SAMPLES), unit_rows.dtype), unit_rows, jnp.zeros((pair_count, frame_len - TEMPLATE_LENGTH), unit_rows.dtype)], axis=1)
    padded_len = BLOCK_SAMPLES + frame_len
    repeated = jnp.tile(padded, (1, BLOCK_SAMPLES + 2))[:, :(BLOCK_SAMPLES + 1) * (padded_len + 1)]
    repeated = repeated.reshape(pair_count, BLOCK_SAMPLES + 1, padded_len + 1)[:, :, :frame_len]
    return repeated[:, 1:][:, ::-1]

def reference(waveform, templates, channel, moveout):
    levels_all = sliding_levels(waveform)
    raw_rows = templates.astype(jnp.float32)
    unit_all = (raw_rows / jnp.sqrt(lax.optimization_barrier(jnp.mean(raw_rows * raw_rows, axis=-1, keepdims=True)) + 1e-05)).astype(jnp.bfloat16)
    segment_len = STAT_SAMPLES + (FRAME_BLOCKS - 1) * BLOCK_SAMPLES
    count_of_blocks = STAT_SAMPLES // BLOCK_SAMPLES

    def template_stat(inputs):
        unit_rows, chan_rows, offsets = inputs
        offsets = offsets.astype(jnp.int32)
        segment_list = jax.vmap(lambda one_row, offset: lax.dynamic_slice_in_dim(one_row, offset, segment_len))(waveform[chan_rows], offsets).astype(jnp.float32)
        block_list = segment_list.reshape(TEMPLATE_CHANS, count_of_blocks + FRAME_BLOCKS - 1, BLOCK_SAMPLES)
        frame_list = jnp.concatenate([block_list[:, block_lag:block_lag + count_of_blocks] for block_lag in range(FRAME_BLOCKS)], axis=-1)
        frequency_band = band_matrix(unit_rows.astype(jnp.float32))
        cross_correlation = jnp.einsum('rgs,rds->rgd', frame_list, frequency_band, precision=lax.Precision.HIGHEST).reshape(TEMPLATE_CHANS, STAT_SAMPLES)
        row_norms = jax.vmap(lambda one_row, offset: lax.dynamic_slice_in_dim(one_row, offset, STAT_SAMPLES))(levels_all[chan_rows], offsets)
        return lax.optimization_barrier(jnp.sum(cross_correlation * row_norms, axis=0)) / math.sqrt(TEMPLATE_LENGTH * TEMPLATE_CHANS)
    return lax.map(template_stat, (unit_all, channel, moveout))
```

```python
import functools, math
import jax, jax.numpy as jnp
from jax import lax
from jax.experimental import pallas as pl
from jax.experimental.pallas import tpu as pltpu
from jax.sharding import PartitionSpec as P

F32, BF16, I32 = jnp.float32, jnp.bfloat16, jnp.int32
TAPS, HALF, LANES = 400, 64, 128
CH, CHP = 75, 80
ROWS, PICK, SLOT = 40, 10, 15

def nt(a, b):
    return lax.dot_general(a, b, (((1,), (1,)), ((), ())), preferred_element_type=F32)

def nn(a, b):
    return jnp.dot(a, b, preferred_element_type=F32)

def iota(shape, d):
    return lax.broadcasted_iota(I32, shape, d)

def pair_lists(first, chan, move):
    n, s = chan.shape
    loc = jnp.where((chan >= first) & (chan < first + CH), 1.0, 0.0).astype(BF16)
    before = jnp.where(iota((s, s), 0) < iota((s, s), 1), 1.0, 0.0).astype(BF16)
    slot_rank = nn(loc, before)
    count = nt(jnp.ones((16, s), BF16), loc)
    here = jnp.where(count > 0.5, 1.0, 0.0).astype(BF16)
    before_t = jnp.where(iota((n, n), 0) < iota((n, n), 1), 1.0, 0.0).astype(BF16)
    rank = nn(here, before_t).astype(I32)
    sel = jnp.where((rank == iota((16, n), 0)) & (count > 0.5), 1.0, 0.0).astype(BF16)
    keep = lambda v: jnp.where((chan >= first) & (chan < first + CH), v, 0).astype(F32).astype(BF16)
    cl = nn(sel, keep(chan - first))
    hi = nn(sel, keep(move // LANES))
    lo = nn(sel, keep(move % LANES))
    kk = nn(sel, keep(iota((n, s), 0)))
    lsel = nn(sel, loc)
    rsel = nn(sel, slot_rank.astype(BF16)).astype(I32)
    eq = (rsel[:, None, :] == iota((16, 16, s), 1)) & (lsel[:, None, :] > 0.5)
    eq = jnp.where(eq, 1.0, 0.0).reshape(256, s).astype(BF16)
    diag = iota((16, 256), 0) == iota((16, 256), 1) // 16
    rows = []
    for v in (cl, hi, lo, kk):
        full = nt(v.astype(BF16), eq)
        rows.append(jnp.sum(jnp.where(diag, full, 0.0), axis=0, keepdims=True))
    scal = jnp.concatenate(rows + rows, axis=0).astype(I32)
    return scal, eq

def kernel(x_ref, t_ref, ch_ref, mv_ref, o_ref, scal_v, scal, eq_ref, band, xs, frames, lev, rolled, sem, *, parts, merge):
    first = lax.axis_index("sta") * CH
    sc, eq = pair_lists(first, ch_ref[...], mv_ref[...])
    scal_v[...] = sc
    eq_ref[...] = eq.astype(F32)
    cp = pltpu.make_async_copy(scal_v, scal, sem)
    cp.start(); cp.wait()

    if "b" in parts:
        @pl.loop(0, PICK)
        def _(i):
            k = scal[3, i * 16]
            pick = nn(eq_ref[pl.ds(i * 16, 16), :].astype(BF16), t_ref[k])
            unit = pick / jnp.sqrt(jnp.sum(pick * pick, axis=1, keepdims=True) / TAPS + 1e-5)
            unit = unit.astype(BF16).astype(F32)
            unit = jnp.concatenate([unit, jnp.zeros((16, 512 - TAPS), F32)], axis=1)
            for j in range(SLOT):
                row = jnp.broadcast_to(unit[j:j + 1, :], (HALF, 512))
                b = pltpu.roll(row, 0, 1, stride=1, stride_axis=0)
                band[i * SLOT + j] = b.astype(BF16)

    if "x" in parts:
        lane = iota((CHP, LANES), 1)
        @pl.loop(0, ROWS)
        def _(g):
            a = x_ref[g].astype(F32)
            b = x_ref[jnp.minimum(g + 1, ROWS - 1)].astype(F32)
            xs[0, g] = a
            xs[1, g] = pltpu.roll(jnp.where(lane < HALF, b, a), HALF, 1)
        e, d = iota((640, LANES), 0), iota((640, LANES), 1)
        window = jnp.where((e >= d) & (e < d + TAPS), 1.0, 0.0).astype(BF16)
        factor = 1.0 / math.sqrt(TAPS * 30)
        @pl.loop(0, 36)
        def _(g):
            sq = jnp.concatenate([(xs[0, g + q] * xs[0, g + q]).astype(BF16) for q in range(5)], axis=1)
            s = nn(sq, window)
            lev[g] = lax.rsqrt(s / TAPS + 1e-5) * factor
        xf = xs.reshape(2 * 44 * CHP, LANES)
        @pl.loop(0, CH)
        def _(c):
            for h in range(2):
                for q in range(4):
                    v = xf[pl.ds(c + (h * 44 + q) * CHP, ROWS, stride=CHP), :]
                    frames[c, pl.ds(h * ROWS, ROWS), pl.ds(q * LANES, LANES)] = v.astype(BF16)

    if "m" in parts:
        levf = lev.reshape(ROWS * CHP, LANES)
        lane = iota((32, LANES), 1)
        lane40 = iota((ROWS, LANES), 1)
        @pl.loop(0, PICK)
        def _(i):
            acc = jnp.zeros((32, LANES), F32)
            for j in range(SLOT):
                p = i * 16 + j
                c, a, r = scal[0, p], scal[1, p], scal[2, p]
                b = band[i * SLOT + j]
                if merge == "dup":
                    y = nt(frames[c], jnp.concatenate([b, b], axis=0))
                    y = jnp.where(lane40 < HALF, y[:ROWS], y[ROWS:])
                elif merge == "cat":
                    y = nt(frames[c], b)
                    y = jnp.concatenate([y[:ROWS], y[ROWS:]], axis=1)
                w = y * levf[pl.ds(c, ROWS, stride=CHP), :]
                rolled[j] = pltpu.roll(w, (LANES - r) % LANES, 1)
                acc += jnp.where(lane < LANES - r, rolled[j, pl.ds(a, 32), :], rolled[j, pl.ds(a + 1, 32), :])
            o_ref[i] = acc

def call(x, t, ch, mv, parts="bxm", merge="cat"):
    vm = pl.BlockSpec(memory_space=pltpu.VMEM)
    return pl.pallas_call(
        functools.partial(kernel, parts=parts, merge=merge),
        out_shape=jax.ShapeDtypeStruct((PICK, 32, LANES), F32),
        in_specs=[vm] * 4, out_specs=vm,
        scratch_shapes=[
            pltpu.VMEM((8, 256), I32), pltpu.SMEM((8, 256), I32), pltpu.VMEM((256, 30), F32),
            pltpu.VMEM((PICK * SLOT, HALF, 512), BF16),
            pltpu.VMEM((2, 44, CHP, LANES), F32),
            pltpu.VMEM((CHP, 2 * ROWS, 512), BF16),
            pltpu.VMEM((ROWS, CHP, LANES), F32),
            pltpu.VMEM((SLOT, ROWS, LANES), F32),
            pltpu.SemaphoreType.DMA(()),
        ],
        compiler_params=pltpu.CompilerParams(vmem_limit_bytes=56 << 20),
    )(x, t, ch, mv)


def combine(blocks, channel):
    home = channel // CH
    groups = jnp.arange(16, dtype=I32)
    here = jnp.any(home[None] == groups[:, None, None], axis=2)
    rank = jnp.cumsum(here.astype(I32), axis=1) - 1
    pick = here[:, :, None] & (rank[:, :, None] == jnp.arange(PICK, dtype=I32))
    pick = pick.transpose(1, 0, 2).reshape(channel.shape[0], 16 * PICK).astype(F32)
    return jnp.dot(pick, blocks.reshape(16 * PICK, 256), precision=lax.Precision.HIGHEST)


def shards(waveform, templates, channel, moveout):
    gathered = lax.all_gather(waveform, "tmpl", axis=1, tiled=True)
    x = gathered.reshape(CH, ROWS, LANES).transpose(1, 0, 2)
    x = jnp.pad(x, ((0, 0), (0, CHP - CH), (0, 0)))
    rows = call(x, templates, channel, moveout)
    rows = rows.reshape(PICK, 16, 256).transpose(1, 0, 2)
    blocks = lax.all_to_all(rows, "sta", 0, 0)
    return combine(blocks, channel)


def solution(mesh):
    placed = (P("sta", "tmpl"), P("tmpl", None, None), P("tmpl", None), P("tmpl", None))
    return jax.shard_map(
        shards, mesh=mesh, in_specs=placed, out_specs=P("tmpl", "sta"), check_vma=False
    )
```

```python
import math

import jax
import jax.numpy as jnp
from jax import lax
from jax.experimental import pallas as pl
from jax.experimental.pallas import tpu as pltpu
from jax.sharding import PartitionSpec as P

F32, BF16, I32 = jnp.float32, jnp.bfloat16, jnp.int32
TAPS = 400
LANES = 128
HALF = 64
WIDE = 512
CH, CHP = 75, 80
PITCH = 84
ROWS = 40
USED = 36
PICK, SLOT = 10, 15
Z, Y, CHUNK = 8, 4, 5
GROUPS = 16
BATCH, EACH = 2, 5


def nt(a, b):
    return lax.dot_general(a, b, (((1,), (1,)), ((), ())), preferred_element_type=F32)


def nn(a, b):
    return jnp.dot(a, b, preferred_element_type=F32)


def iota(shape, d):
    return lax.broadcasted_iota(I32, shape, d)


def ones_where(cond):
    return jnp.where(cond, 1.0, 0.0).astype(BF16)


def pair_lists(first, chan, move):
    n, s = chan.shape
    inside = (chan >= first) & (chan < first + CH)
    loc = ones_where(inside)
    slot_rank = nn(loc, ones_where(iota((s, s), 0) < iota((s, s), 1)))
    count = nt(jnp.ones((16, s), BF16), loc)
    rank = nn(ones_where(count > 0.5), ones_where(iota((n, n), 0) < iota((n, n), 1))).astype(I32)
    sel = ones_where((rank == iota((16, n), 0)) & (count > 0.5))

    def keep(v):
        return nn(sel, jnp.where(inside, v, 0).astype(F32).astype(BF16))

    cols = (keep(chan - first), keep(move // LANES), keep(move % LANES), keep(iota((n, s), 0)))
    lsel = nn(sel, loc)
    rsel = nn(sel, slot_rank.astype(BF16)).astype(I32)
    eq = (rsel[:, None, :] == iota((16, 16, s), 1)) & (lsel[:, None, :] > 0.5)
    eq3 = jnp.where(eq, 1.0, 0.0)
    eq = eq3.reshape(256, s).astype(BF16)
    diag = iota((16, 256), 0) == iota((16, 256), 1) // 16
    rows = []
    for v in cols:
        rows.append(jnp.sum(jnp.where(diag, nt(v.astype(BF16), eq), 0.0), axis=0, keepdims=True))
    place = jnp.sum(eq3 * (iota((16, 16, s), 2).astype(F32) * n + cols[3][:, None, :] + 1.0), axis=2, keepdims=True)
    return jnp.concatenate(rows + rows, axis=0).astype(I32), place.reshape(256, 1) - 1.0


def combine_rows(chan, half):
    n = chan.shape[0]
    grp = chan // CH
    low = jnp.min(grp, axis=1, keepdims=True)
    high = jnp.max(grp, axis=1, keepdims=True)
    lane = iota((n, BATCH * 256), 1)
    batch, group, part, row = lane // 256, lane % 256 // 16, lane % 16 // 8, lane % 8
    here = (group == low) | (group == high)
    rank = nn(ones_where(iota((n, n), 1) < iota((n, n), 0)), ones_where(here)).astype(I32)
    hit = here & (part == half) & (row < EACH) & (rank == batch * EACH + row)
    return jnp.where(hit, 1.0, 0.0)


def kernel(w_ref, t_hbm, ch_ref, mv_ref, o_ref,
           wide, ybuf, x_all, t_ref, scal_v, scal, units, band, xs, sqs, frames, lev, rolled, outbox, inbox,
           y_send, y_recv, z_send, z_recv, a_send, a_recv, t_sem, s_sem):
    tm, st = lax.axis_index("tmpl"), lax.axis_index("sta")
    zz, yy = tm // Y, tm % Y
    up, down = (tm + Y) % (Z * Y), (tm + Z * Y - Y) % (Z * Y)
    y_peer = [zz * Y + (yy + d) % Y for d in range(1, Y)]
    s_peer = [(st + d) % GROUPS for d in range(1, GROUPS)]

    barrier = pltpu.get_barrier_semaphore()
    for p in y_peer + [up, down]:
        pl.semaphore_signal(barrier, inc=1, device_id={"tmpl": p}, device_id_type=pl.DeviceIdType.MESH)
    for p in s_peer:
        pl.semaphore_signal(barrier, inc=1, device_id={"sta": p}, device_id_type=pl.DeviceIdType.MESH)

    t_copy = pltpu.make_async_copy(t_hbm, t_ref, t_sem)
    t_copy.start()

    wide[...] = jnp.zeros_like(wide)
    wide[pl.ds(0, CH), pl.ds(0, 160)] = w_ref[...].astype(F32)
    own = pltpu.roll(wide[...], 32 * yy, 1)
    own = jnp.concatenate([own[:, :LANES], own[:, LANES:]], axis=0).astype(BF16)
    ybuf[yy] = own
    outbox[...] = jnp.zeros_like(outbox)

    pl.semaphore_wait(barrier, Y - 1 + 2 + GROUPS - 1)

    y_copies = []
    for d in range(1, Y):
        cp = pltpu.make_async_remote_copy(
            src_ref=ybuf.at[yy], dst_ref=ybuf.at[yy], send_sem=y_send.at[d - 1], recv_sem=y_recv.at[d - 1],
            device_id={"tmpl": y_peer[d - 1]}, device_id_type=pl.DeviceIdType.MESH)
        cp.start()
        y_copies.append(cp)

    sc, place = pair_lists(st * CH, ch_ref[...], mv_ref[...])
    scal_v[...] = sc
    s_copy = pltpu.make_async_copy(scal_v, scal, s_sem)
    s_copy.start()

    for cp in y_copies:
        cp.wait()
    parts = [ybuf[y].astype(F32) for y in range(Y)]
    for n in range(CHUNK):
        v = 0.0
        if n < Y:
            v += parts[n][:CHP]
        if n > 0:
            v += parts[n - 1][CHP:]
        x_all[zz * CHUNK + n] = v.astype(BF16)

    def ring(step, direction):
        src = (zz + Z - step) % Z if direction == 0 else (zz + step) % Z
        first, count = (0, CHUNK) if step < 3 else ((0, 3) if direction == 0 else (3, 2))
        piece = x_all.at[pl.ds(src * CHUNK + first, count)]
        return pltpu.make_async_remote_copy(
            src_ref=piece, dst_ref=piece, send_sem=z_send.at[direction, step], recv_sem=z_recv.at[direction, step],
            device_id={"tmpl": up if direction == 0 else down}, device_id_type=pl.DeviceIdType.MESH)

    steps = [[ring(s, d) for d in range(2)] for s in range(4)]
    for cp in steps[0]:
        cp.start()

    t_copy.wait()
    s_copy.wait()

    slots, count = t_ref.shape[:2]
    rows = t_ref[...].reshape(slots * count, TAPS)
    pick = nn(ones_where(place[:16 * PICK].astype(I32) == iota((16 * PICK, slots * count), 1)), rows)
    unit = pick / jnp.sqrt(jnp.sum(pick * pick, axis=1, keepdims=True) / TAPS + 1e-5)
    unit = unit.astype(BF16).astype(F32)
    units[...] = jnp.concatenate([unit, jnp.zeros((16 * PICK, WIDE - TAPS), F32)], axis=1)

    def bands(lo, hi):
        @pl.loop(lo, hi)
        def _(i):
            unit = units[pl.ds(pl.multiple_of(i * 16, 16), 16), :]
            for j in range(SLOT):
                row = jnp.broadcast_to(unit[j:j + 1, :], (HALF, WIDE))
                band[i * SLOT + j] = pltpu.roll(row, 0, 1, stride=1, stride_axis=0).astype(BF16)

    cuts = (0, 3, 6, 9, 10)
    for s in range(4):
        bands(cuts[s], cuts[s + 1])
        for d in range(2):
            steps[s][d].wait()
            if s < 3:
                steps[s + 1][d].start()

    lane = iota((CHP, LANES), 1)

    @pl.loop(0, Z)
    def _(z):
        rows = [x_all[z * CHUNK + n] for n in range(CHUNK)] + [x_all[jnp.minimum(z * CHUNK + CHUNK, ROWS - 1)]]
        rows = [v.astype(F32) for v in rows]
        for n in range(CHUNK):
            g = z * CHUNK + n
            xs[pl.ds(g * PITCH, CHP), :] = rows[n]
            xs[pl.ds((ROWS + 4 + g) * PITCH, CHP), :] = pltpu.roll(jnp.where(lane < HALF, rows[n + 1], rows[n]), HALF, 1)
            sqs[pl.ds(pl.multiple_of(g * CHP, CHP), CHP), :] = (rows[n] * rows[n]).astype(BF16)

    e, d = iota((5 * LANES, LANES), 0), iota((5 * LANES, LANES), 1)
    window = ones_where((e >= d) & (e < d + TAPS))
    factor = 1.0 / math.sqrt(TAPS * 2 * SLOT)
    many = 9

    @pl.loop(0, USED // many)
    def _(t):
        base = t * (many * CHP)
        s = 0.0
        for q in range(5):
            rows = sqs[pl.ds(pl.multiple_of(base + q * CHP, CHP), many * CHP), :]
            s += nn(rows, window[q * LANES:(q + 1) * LANES])
        s = lax.rsqrt(s / TAPS + 1e-5) * factor
        for n in range(many):
            lev[pl.ds((t * many + n) * PITCH, CHP), :] = s[n * CHP:(n + 1) * CHP]

    @pl.loop(0, CH)
    def _(c):
        for h in range(2):
            for q in range(4):
                v = xs[pl.ds(c + (h * (ROWS + 4) + q) * PITCH, ROWS, stride=PITCH), :]
                frames[c, pl.ds(h * ROWS, ROWS), pl.ds(q * LANES, LANES)] = v.astype(BF16)

    lane32 = iota((32, LANES), 1)

    def stacks(b):
        @pl.loop(0, EACH)
        def _(ii):
            i = b * EACH + ii
            acc = jnp.zeros((32, LANES), F32)
            for j in range(SLOT):
                p = i * 16 + j
                c, a, r = (jnp.clip(scal[n, p], 0, top) for n, top in enumerate((CH - 1, 3, LANES - 1)))
                y = nt(frames[c], band[i * SLOT + j])
                y = jnp.concatenate([y[:ROWS], y[ROWS:]], axis=1)
                rolled[j] = pltpu.roll(y * lev[pl.ds(c, ROWS, stride=PITCH), :], (LANES - r) % LANES, 1)
                acc += jnp.where(lane32 < LANES - r, rolled[j, pl.ds(a, 32), :], rolled[j, pl.ds(a + 1, 32), :])
            outbox[b, pl.ds(ii, 32, stride=8), :] = acc

    sends = []
    for b in range(BATCH):
        stacks(b)
        for d in range(1, GROUPS):
            cp = pltpu.make_async_remote_copy(
                src_ref=outbox.at[b, pl.ds(s_peer[d - 1] * 16, 16)], dst_ref=inbox.at[b, pl.ds(st * 16, 16)],
                send_sem=a_send.at[b, d - 1], recv_sem=a_recv.at[b, d - 1],
                device_id={"sta": s_peer[d - 1]}, device_id_type=pl.DeviceIdType.MESH)
            cp.start()
            sends.append(cp)
        inbox[b, pl.ds(st * 16, 16), :] = outbox[b, pl.ds(st * 16, 16), :]

    hits = [combine_rows(ch_ref[...], h) for h in range(2)]
    for cp in sends:
        cp.wait()
    rows = inbox[...].reshape(BATCH * 256, LANES)
    for h in range(2):
        o_ref[:, pl.ds(h * LANES, LANES)] = jnp.dot(
            hits[h], rows, precision=lax.Precision.HIGHEST, preferred_element_type=F32)


def shards(waveform, templates, channel, moveout):
    vm = pl.BlockSpec(memory_space=pltpu.VMEM)
    sem = pltpu.SemaphoreType.DMA
    templates = templates.transpose(1, 0, 2)
    return pl.pallas_call(
        kernel,
        out_shape=jax.ShapeDtypeStruct((templates.shape[1], 2 * LANES), F32),
        in_specs=[vm, pl.BlockSpec(memory_space=pl.ANY), vm, vm],
        out_specs=vm,
        scratch_shapes=[
            pltpu.VMEM((CHP, 2 * LANES), F32),
            pltpu.VMEM((Y, 2 * CHP, LANES), BF16),
            pltpu.VMEM((ROWS, CHP, LANES), BF16),
            pltpu.VMEM(templates.shape, BF16),
            pltpu.VMEM((8, 256), I32),
            pltpu.SMEM((8, 256), I32),
            pltpu.VMEM((16 * PICK, WIDE), F32),
            pltpu.VMEM((PICK * SLOT, HALF, WIDE), BF16),
            pltpu.VMEM((2 * (ROWS + 4) * PITCH + CHP, LANES), F32),
            pltpu.VMEM((ROWS * CHP, LANES), BF16),
            pltpu.VMEM((CHP, 2 * ROWS, WIDE), BF16),
            pltpu.VMEM((ROWS * PITCH + CHP, LANES), F32),
            pltpu.VMEM((SLOT, ROWS, LANES), F32),
            pltpu.VMEM((BATCH, 264, LANES), F32),
            pltpu.VMEM((BATCH, 256, LANES), F32),
            sem((Y - 1,)), sem((Y - 1,)), sem((2, 4)), sem((2, 4)),
            sem((BATCH, GROUPS - 1)), sem((BATCH, GROUPS - 1)), sem(()), sem(()),
        ],
        compiler_params=pltpu.CompilerParams(
            vmem_limit_bytes=56 << 20, collective_id=0, has_side_effects=True
        ),
    )(waveform, templates, channel, moveout)


def solution(mesh):
    placed = (P("sta", "tmpl"), P("tmpl", None, None), P("tmpl", None), P("tmpl", None))
    return jax.shard_map(
        shards, mesh=mesh, in_specs=placed, out_specs=P("tmpl", "sta"), check_vma=False
    )
```

```python
import math

import jax
import jax.numpy as jnp
from jax import lax
from jax.experimental import pallas as pl
from jax.experimental.pallas import tpu as pltpu
from jax.sharding import PartitionSpec as P

F32, BF16, I32 = jnp.float32, jnp.bfloat16, jnp.int32
TAPS = 400
LANES = 128
HALF = 64
WIDE = 512
CH, CHP = 75, 80
PITCH = 84
ROWS = 40
PICK, SLOT = 10, 15
Z, Y, CHUNK = 8, 4, 5
GROUPS = 16
BATCH, EACH = 2, 5


def nt(a, b):
    return lax.dot_general(a, b, (((1,), (1,)), ((), ())), preferred_element_type=F32)


def nn(a, b):
    return jnp.dot(a, b, preferred_element_type=F32)


def iota(shape, d):
    return lax.broadcasted_iota(I32, shape, d)


def ones_where(cond):
    return jnp.where(cond, 1.0, 0.0).astype(BF16)


def pair_lists(first, chan, move):
    n, s = chan.shape
    inside = (chan >= first) & (chan < first + CH)
    loc = ones_where(inside)
    slot_rank = nn(loc, ones_where(iota((s, s), 0) < iota((s, s), 1)))
    count = nt(jnp.ones((16, s), BF16), loc)
    rank = nn(ones_where(count > 0.5), ones_where(iota((n, n), 0) < iota((n, n), 1))).astype(I32)
    sel = ones_where((rank == iota((16, n), 0)) & (count > 0.5))

    def keep(v):
        return nn(sel, jnp.where(inside, v, 0).astype(F32).astype(BF16))

    cols = (keep(chan - first), keep(move // LANES), keep(move % LANES), keep(iota((n, s), 0)))
    lsel = nn(sel, loc)
    rsel = nn(sel, slot_rank.astype(BF16)).astype(I32)
    eq = (rsel[:, None, :] == iota((16, 16, s), 1)) & (lsel[:, None, :] > 0.5)
    eq3 = jnp.where(eq, 1.0, 0.0)
    eq = eq3.reshape(256, s).astype(BF16)
    diag = iota((16, 256), 0) == iota((16, 256), 1) // 16
    rows = []
    for v in cols:
        rows.append(jnp.sum(jnp.where(diag, nt(v.astype(BF16), eq), 0.0), axis=0, keepdims=True))
    place = jnp.sum(eq3 * (iota((16, 16, s), 2).astype(F32) * n + cols[3][:, None, :] + 1.0), axis=2, keepdims=True)
    return jnp.concatenate(rows + rows, axis=0).astype(I32), place.reshape(256, 1) - 1.0


def combine_rows(chan, half):
    n = chan.shape[0]
    grp = chan // CH
    low = jnp.min(grp, axis=1, keepdims=True)
    high = jnp.max(grp, axis=1, keepdims=True)
    lane = iota((n, BATCH * 256), 1)
    batch, group, part, row = lane // 256, lane % 256 // 16, lane % 16 // 8, lane % 8
    here = (group == low) | (group == high)
    rank = nn(ones_where(iota((n, n), 1) < iota((n, n), 0)), ones_where(here)).astype(I32)
    hit = here & (part == half) & (row < EACH) & (rank == batch * EACH + row)
    return jnp.where(hit, 1.0, 0.0)


def kernel(w_ref, t_hbm, ch_ref, mv_ref, o_ref,
           wide, ybuf, x_all, t_ref, scal_v, scal, units, band, xs, sqs, frames, lev, rolled, outbox, inbox,
           y_send, y_recv, z_send, z_recv, a_send, a_recv, t_sem, s_sem):
    tm, st = lax.axis_index("tmpl"), lax.axis_index("sta")
    zz, yy = tm // Y, tm % Y
    z_peer = {d: (tm + (Z + d) * Y) % (Z * Y) for d in (1, -1, 2, -2)}
    y_peer = [zz * Y + (yy + d) % Y for d in range(1, Y)]
    s_peer = [(st + d) % GROUPS for d in range(1, GROUPS)]

    barrier = pltpu.get_barrier_semaphore()
    for p in y_peer + list(z_peer.values()):
        pl.semaphore_signal(barrier, inc=1, device_id={"tmpl": p}, device_id_type=pl.DeviceIdType.MESH)
    for p in s_peer:
        pl.semaphore_signal(barrier, inc=1, device_id={"sta": p}, device_id_type=pl.DeviceIdType.MESH)

    t_copy = pltpu.make_async_copy(t_hbm, t_ref, t_sem)
    t_copy.start()

    wide[...] = jnp.zeros_like(wide)
    wide[pl.ds(0, CH), pl.ds(0, 160)] = w_ref[...].astype(F32)
    own = pltpu.roll(wide[...], 32 * yy, 1)
    own = jnp.concatenate([own[:, :LANES], own[:, LANES:]], axis=0).astype(BF16)
    ybuf[yy] = own
    outbox[...] = jnp.zeros_like(outbox)

    pl.semaphore_wait(barrier, Y - 1 + 4 + GROUPS - 1)

    y_copies = []
    for d in range(1, Y):
        cp = pltpu.make_async_remote_copy(
            src_ref=ybuf.at[yy], dst_ref=ybuf.at[yy], send_sem=y_send.at[d - 1], recv_sem=y_recv.at[d - 1],
            device_id={"tmpl": y_peer[d - 1]}, device_id_type=pl.DeviceIdType.MESH)
        cp.start()
        y_copies.append(cp)

    sc, place = pair_lists(st * CH, ch_ref[...], mv_ref[...])
    scal_v[...] = sc
    s_copy = pltpu.make_async_copy(scal_v, scal, s_sem)
    s_copy.start()

    for cp in y_copies:
        cp.wait()
    parts = [ybuf[y].astype(F32) for y in range(Y)]
    for n in range(CHUNK):
        v = 0.0
        if n < Y:
            v += parts[n][:CHP]
        if n > 0:
            v += parts[n - 1][CHP:]
        x_all[n] = v.astype(BF16)

    def pass_on(n, chunk, d, first=0, count=CHUNK):
        there = (chunk - d) % Z
        return pltpu.make_async_remote_copy(
            src_ref=x_all.at[pl.ds(chunk % Z * CHUNK + first, count)],
            dst_ref=x_all.at[pl.ds(there * CHUNK + first, count)],
            send_sem=z_send.at[n], recv_sem=z_recv.at[n],
            device_id={"tmpl": z_peer[d]}, device_id_type=pl.DeviceIdType.MESH)

    from_two = [pass_on(0, 0, 2), pass_on(1, 0, -2)]
    from_one = [pass_on(2, 0, 1), pass_on(3, 0, -1)]
    from_four = [pass_on(4, -2, 2, 0, 3), pass_on(5, 2, -2, 3, 2)]
    from_three = [pass_on(6, -2, 1), pass_on(7, 2, -1)]
    for cp in from_two + from_one:
        cp.start()

    t_copy.wait()
    s_copy.wait()

    slots, count = t_ref.shape[:2]
    rows = t_ref[...].reshape(slots * count, TAPS)
    pick = nn(ones_where(place[:16 * PICK].astype(I32) == iota((16 * PICK, slots * count), 1)), rows)
    unit = pick / jnp.sqrt(jnp.sum(pick * pick, axis=1, keepdims=True) / TAPS + 1e-5)
    unit = unit.astype(BF16).astype(F32)
    units[...] = jnp.concatenate([unit, jnp.zeros((16 * PICK, WIDE - TAPS), F32)], axis=1)

    def bands(lo, hi):
        @pl.loop(lo, hi)
        def _(i):
            unit = units[pl.ds(pl.multiple_of(i * 16, 16), 16), :]
            for j in range(SLOT):
                row = jnp.broadcast_to(unit[j:j + 1, :], (HALF, WIDE))
                band[i * SLOT + j] = pltpu.roll(row, 0, 1, stride=1, stride_axis=0).astype(BF16)

    lane = iota((CHP, LANES), 1)

    def put(g, row, odd):
        xs[pl.ds((g + odd * (ROWS + 4)) * PITCH, CHP), :] = row

    def take(c):
        rows = [x_all[c * CHUNK + n].astype(F32) for n in range(CHUNK)]
        for n in range(CHUNK):
            again = (0, ROWS) if c == 0 and n < 4 else (0,)
            later = pltpu.roll(jnp.where(lane < HALF, rows[n + 1], rows[n]), HALF, 1) if n < CHUNK - 1 else None
            square = (rows[n] * rows[n]).astype(BF16)
            for more in again:
                g = c * CHUNK + n + more
                put(g, rows[n], 0)
                if later is not None:
                    put(g, later, 1)
                sqs[pl.ds(g * CHP, CHP), :] = square

    e, d = iota((5 * LANES, LANES), 0), iota((5 * LANES, LANES), 1)
    window = ones_where((e >= d) & (e < d + TAPS))
    factor = 1.0 / math.sqrt(TAPS * 2 * SLOT)
    many = 10

    def levels(g):
        s = 0.0
        for q in range(5):
            s += nn(sqs[pl.ds((g + q) * CHP, many * CHP), :], window[q * LANES:(q + 1) * LANES])
        s = lax.rsqrt(s / TAPS + 1e-5) * factor
        for n in range(many):
            lev[pl.ds((g + n) * PITCH, CHP), :] = s[n * CHP:(n + 1) * CHP]

    bands(0, 5)
    for near, far, one in zip(from_two, from_four, from_three):
        near.wait_recv()
        far.start()
        one.start()
    bands(5, PICK)
    for c in (0, 2, 6):
        take(c)
    for cp in from_one:
        cp.wait_recv()
    for c in (1, 7):
        take(c)
    levels(0)
    levels(30)
    for cp in from_three:
        cp.wait_recv()
    for c in (3, 5):
        take(c)
    for cp in from_four:
        cp.wait_recv()
    take(4)
    for c in range(Z):
        g = c * CHUNK + CHUNK - 1
        first, second = x_all[g].astype(F32), x_all[(g + 1) % ROWS].astype(F32)
        put(g, pltpu.roll(jnp.where(lane < HALF, second, first), HALF, 1), 1)
    levels(10)
    levels(20)

    @pl.loop(0, CH)
    def _(c):
        for h in range(2):
            for q in range(4):
                v = xs[pl.ds(c + (h * (ROWS + 4) + q) * PITCH, ROWS, stride=PITCH), :]
                frames[c, pl.ds(h * ROWS, ROWS), pl.ds(q * LANES, LANES)] = v.astype(BF16)

    start = (ROWS - CHUNK * zz) % ROWS
    lane32 = iota((32, LANES), 1)

    def stacks(b):
        @pl.loop(0, EACH)
        def _(ii):
            i = b * EACH + ii
            acc = jnp.zeros((32, LANES), F32)
            for j in range(SLOT):
                p = i * 16 + j
                c, a, r = (jnp.clip(scal[n, p], 0, top) for n, top in enumerate((CH - 1, 3, LANES - 1)))
                y = nt(frames[c], band[i * SLOT + j])
                y = jnp.concatenate([y[:ROWS], y[ROWS:]], axis=1)
                w = pltpu.roll(y * lev[pl.ds(c, ROWS, stride=PITCH), :], (LANES - r) % LANES, 1)
                rolled[j, pl.ds(0, ROWS), :] = w
                rolled[j, pl.ds(ROWS, 32), :] = w[:32]
                here, after = rolled[j, pl.ds(start + a, 32), :], rolled[j, pl.ds(start + a + 1, 32), :]
                acc += jnp.where(lane32 < LANES - r, here, after)
            outbox[b, pl.ds(ii, 32, stride=8), :] = acc

    sends = []
    for b in range(BATCH):
        stacks(b)
        for d in range(1, GROUPS):
            cp = pltpu.make_async_remote_copy(
                src_ref=outbox.at[b, pl.ds(s_peer[d - 1] * 16, 16)], dst_ref=inbox.at[b, pl.ds(st * 16, 16)],
                send_sem=a_send.at[b, d - 1], recv_sem=a_recv.at[b, d - 1],
                device_id={"sta": s_peer[d - 1]}, device_id_type=pl.DeviceIdType.MESH)
            cp.start()
            sends.append(cp)
        inbox[b, pl.ds(st * 16, 16), :] = outbox[b, pl.ds(st * 16, 16), :]

    hits = [combine_rows(ch_ref[...], h) for h in range(2)]
    total = [0.0, 0.0]
    for b in range(BATCH):
        for cp in sends[b * (GROUPS - 1):(b + 1) * (GROUPS - 1)]:
            cp.wait_recv()
        for h in range(2):
            total[h] += jnp.dot(hits[h][:, b * 256:(b + 1) * 256], inbox[b],
                                precision=lax.Precision.HIGHEST, preferred_element_type=F32)
    for h in range(2):
        o_ref[:, pl.ds(h * LANES, LANES)] = total[h]
    for cp in from_two + from_one + from_four + from_three + sends:
        cp.wait_send()


def shards(waveform, templates, channel, moveout):
    vm = pl.BlockSpec(memory_space=pltpu.VMEM)
    sem = pltpu.SemaphoreType.DMA
    templates = templates.transpose(1, 0, 2)
    return pl.pallas_call(
        kernel,
        out_shape=jax.ShapeDtypeStruct((templates.shape[1], 2 * LANES), F32),
        in_specs=[vm, pl.BlockSpec(memory_space=pl.ANY), vm, vm],
        out_specs=vm,
        scratch_shapes=[
            pltpu.VMEM((CHP, 2 * LANES), F32),
            pltpu.VMEM((Y, 2 * CHP, LANES), BF16),
            pltpu.VMEM((ROWS, CHP, LANES), BF16),
            pltpu.VMEM(templates.shape, BF16),
            pltpu.VMEM((8, 256), I32),
            pltpu.SMEM((8, 256), I32),
            pltpu.VMEM((16 * PICK, WIDE), F32),
            pltpu.VMEM((PICK * SLOT, HALF, WIDE), BF16),
            pltpu.VMEM((2 * (ROWS + 4) * PITCH + CHP, LANES), F32),
            pltpu.VMEM(((ROWS + 4) * CHP, LANES), BF16),
            pltpu.VMEM((CHP, 2 * ROWS, WIDE), BF16),
            pltpu.VMEM((ROWS * PITCH + CHP, LANES), F32),
            pltpu.VMEM((SLOT, ROWS + 32, LANES), F32),
            pltpu.VMEM((BATCH, 264, LANES), F32),
            pltpu.VMEM((BATCH, 256, LANES), F32),
            sem((Y - 1,)), sem((Y - 1,)), sem((8,)), sem((8,)),
            sem((BATCH, GROUPS - 1)), sem((BATCH, GROUPS - 1)), sem(()), sem(()),
        ],
        compiler_params=pltpu.CompilerParams(
            vmem_limit_bytes=56 << 20, collective_id=0, has_side_effects=True
        ),
    )(waveform, templates, channel, moveout)


def solution(mesh):
    placed = (P("sta", "tmpl"), P("tmpl", None, None), P("tmpl", None), P("tmpl", None))
    return jax.shard_map(
        shards, mesh=mesh, in_specs=placed, out_specs=P("tmpl", "sta"), check_vma=False
    )
```

```python
import math

import jax
import jax.numpy as jnp
from jax import lax
from jax.experimental import pallas as pl
from jax.experimental.pallas import tpu as pltpu
from jax.sharding import PartitionSpec as P

F32, BF16, I32 = jnp.float32, jnp.bfloat16, jnp.int32
TAPS = 400
LANES = 128
HALF = 64
WIDE = 512
CH, CHP = 75, 80
PITCH = 84
ROWS = 40
PICK, SLOT = 10, 15
Z, Y, CHUNK = 8, 4, 5
GROUPS = 16
BATCH, EACH = 3, 4
PART = GROUPS * 2 * EACH


def nt(a, b):
    return lax.dot_general(a, b, (((1,), (1,)), ((), ())), preferred_element_type=F32)


def nn(a, b):
    return jnp.dot(a, b, preferred_element_type=F32)


def iota(shape, d):
    return lax.broadcasted_iota(I32, shape, d)


def ones_where(cond):
    return jnp.where(cond, 1.0, 0.0).astype(BF16)


def pair_lists(first, chan, move):
    n, s = chan.shape
    inside = (chan >= first) & (chan < first + CH)
    loc = ones_where(inside)
    slot_rank = nn(loc, ones_where(iota((s, s), 0) < iota((s, s), 1)))
    count = nt(jnp.ones((16, s), BF16), loc)
    rank = nn(ones_where(count > 0.5), ones_where(iota((n, n), 0) < iota((n, n), 1))).astype(I32)
    sel = ones_where((rank == iota((16, n), 0)) & (count > 0.5))

    def keep(v):
        return nn(sel, jnp.where(inside, v, 0).astype(F32).astype(BF16))

    cols = (keep(chan - first), keep(move // LANES), keep(move % LANES), keep(iota((n, s), 0)))
    lsel = nn(sel, loc)
    rsel = nn(sel, slot_rank.astype(BF16)).astype(I32)
    eq = (rsel[:, None, :] == iota((16, 16, s), 1)) & (lsel[:, None, :] > 0.5)
    eq3 = jnp.where(eq, 1.0, 0.0)
    eq = eq3.reshape(256, s).astype(BF16)
    diag = iota((16, 256), 0) == iota((16, 256), 1) // 16
    rows = []
    for v in cols:
        rows.append(jnp.sum(jnp.where(diag, nt(v.astype(BF16), eq), 0.0), axis=0, keepdims=True))
    place = jnp.sum(eq3 * (iota((16, 16, s), 2).astype(F32) * n + cols[3][:, None, :] + 1.0), axis=2, keepdims=True)
    return jnp.concatenate(rows + rows, axis=0).astype(I32), place.reshape(256, 1) - 1.0


def combine_rows(chan, half):
    n = chan.shape[0]
    grp = chan // CH
    low = jnp.min(grp, axis=1, keepdims=True)
    high = jnp.max(grp, axis=1, keepdims=True)
    lane = iota((n, BATCH * PART), 1)
    batch, group, part, row = lane // PART, lane % PART // (2 * EACH), lane % (2 * EACH) // EACH, lane % EACH
    here = (group == low) | (group == high)
    rank = nn(ones_where(iota((n, n), 1) < iota((n, n), 0)), ones_where(here)).astype(I32)
    hit = here & (part == half) & (rank == batch * EACH + row)
    return jnp.where(hit, 1.0, 0.0)


def kernel(w_hbm, t_hbm, ch_hbm, mv_hbm, o_ref,
           w_ref, ch_ref, mv_ref, wide, ybuf, x_all, t_ref, scal_v, scal, units, band, xs, sqs, frames, lev, rolled, outbox, inbox,
           y_send, y_recv, z_send, z_recv, a_send, a_recv, in_sem, s_sem):
    tm, st = lax.axis_index("tmpl"), lax.axis_index("sta")
    zz, yy = tm // Y, tm % Y
    z_peer = {d: (tm + (Z + d) * Y) % (Z * Y) for d in (1, -1, 2, -2)}
    y_peer = [zz * Y + (yy + d) % Y for d in range(1, Y)]
    s_peer = [(st + d) % GROUPS for d in range(1, GROUPS)]

    barrier = pltpu.get_barrier_semaphore()
    for p in y_peer + list(z_peer.values()):
        pl.semaphore_signal(barrier, inc=1, device_id={"tmpl": p}, device_id_type=pl.DeviceIdType.MESH)
    for p in s_peer:
        pl.semaphore_signal(barrier, inc=1, device_id={"sta": p}, device_id_type=pl.DeviceIdType.MESH)

    copies = [pltpu.make_async_copy(src, dst, in_sem.at[n]) for n, (src, dst) in enumerate(
        ((w_hbm, w_ref), (ch_hbm, ch_ref), (mv_hbm, mv_ref), (t_hbm, t_ref)))]
    for cp in copies:
        cp.start()
    outbox[...] = jnp.zeros_like(outbox)

    wide[...] = jnp.zeros_like(wide)
    copies[0].wait()
    wide[pl.ds(0, CH), pl.ds(0, 160)] = w_ref[...].astype(F32)
    own = pltpu.roll(wide[...], 32 * yy, 1)
    own = jnp.concatenate([own[:, :LANES], own[:, LANES:]], axis=0).astype(BF16)
    ybuf[yy] = own

    pl.semaphore_wait(barrier, Y - 1 + 4 + GROUPS - 1)

    y_copies = []
    for d in range(1, Y):
        cp = pltpu.make_async_remote_copy(
            src_ref=ybuf.at[yy], dst_ref=ybuf.at[yy], send_sem=y_send.at[d - 1], recv_sem=y_recv.at[d - 1],
            device_id={"tmpl": y_peer[d - 1]}, device_id_type=pl.DeviceIdType.MESH)
        cp.start()
        y_copies.append(cp)

    copies[1].wait()
    copies[2].wait()
    sc, place = pair_lists(st * CH, ch_ref[...], mv_ref[...])
    scal_v[...] = sc
    s_copy = pltpu.make_async_copy(scal_v, scal, s_sem)
    s_copy.start()

    for cp in y_copies:
        cp.wait()
    parts = [ybuf[y].astype(F32) for y in range(Y)]
    for n in range(CHUNK):
        v = 0.0
        if n < Y:
            v += parts[n][:CHP]
        if n > 0:
            v += parts[n - 1][CHP:]
        x_all[2 * CHUNK + n] = v.astype(BF16)

    def pass_on(n, chunk, d, first=0, count=CHUNK):
        there = (chunk - d) % Z
        return pltpu.make_async_remote_copy(
            src_ref=x_all.at[pl.ds(chunk % Z * CHUNK + first, count)],
            dst_ref=x_all.at[pl.ds(there * CHUNK + first, count)],
            send_sem=z_send.at[n], recv_sem=z_recv.at[n],
            device_id={"tmpl": z_peer[d]}, device_id_type=pl.DeviceIdType.MESH)

    from_two = [pass_on(0, 2, 2), pass_on(1, 2, -2)]
    from_one = [pass_on(2, 2, 1), pass_on(3, 2, -1)]
    from_four = [pass_on(4, 0, 2, 0, 3), pass_on(5, 4, -2, 3, 2)]
    from_three = [pass_on(6, 0, 1), pass_on(7, 4, -1)]
    for cp in from_two + from_one:
        cp.start()

    copies[3].wait()
    s_copy.wait()

    slots, count = t_ref.shape[:2]
    rows = t_ref[...].reshape(slots * count, TAPS)
    pick = nn(ones_where(place[:16 * PICK].astype(I32) == iota((16 * PICK, slots * count), 1)), rows)
    unit = pick / jnp.sqrt(jnp.sum(pick * pick, axis=1, keepdims=True) / TAPS + 1e-5)
    unit = unit.astype(BF16).astype(F32)
    units[...] = jnp.concatenate([unit, jnp.zeros((16 * PICK, WIDE - TAPS), F32)], axis=1)

    def bands(lo, hi):
        @pl.loop(lo, hi)
        def _(i):
            unit = units[pl.ds(pl.multiple_of(i * 16, 16), 16), :]
            for j in range(SLOT):
                row = jnp.broadcast_to(unit[j:j + 1, :], (HALF, WIDE))
                band[i * SLOT + j] = pltpu.roll(row, 0, 1, stride=1, stride_axis=0).astype(BF16)

    lane = iota((CHP, LANES), 1)

    def put(g, row, odd):
        xs[pl.ds((g + odd * (ROWS + 4)) * PITCH, CHP), :] = row

    def take(c):
        rows = [x_all[c * CHUNK + n].astype(F32) for n in range(CHUNK)]
        for n in range(CHUNK):
            again = (0, ROWS) if c == 0 and n < 4 else (0,)
            later = pltpu.roll(jnp.where(lane < HALF, rows[n + 1], rows[n]), HALF, 1) if n < CHUNK - 1 else None
            square = (rows[n] * rows[n]).astype(BF16)
            for more in again:
                g = c * CHUNK + n + more
                put(g, rows[n], 0)
                if later is not None:
                    put(g, later, 1)
                sqs[pl.ds(g * CHP, CHP), :] = square

    e, d = iota((5 * LANES, LANES), 0), iota((5 * LANES, LANES), 1)
    window = ones_where((e >= d) & (e < d + TAPS))
    factor = 1.0 / math.sqrt(TAPS * 2 * SLOT)
    many = 8

    def levels(g):
        s = 0.0
        for q in range(5):
            s += nn(sqs[pl.ds((g + q) * CHP, many * CHP), :], window[q * LANES:(q + 1) * LANES])
        s = lax.rsqrt(s / TAPS + 1e-5) * factor
        for n in range(many):
            lev[pl.ds((g + n) * PITCH, CHP), :] = s[n * CHP:(n + 1) * CHP]

    def join(c):
        g = c * CHUNK + CHUNK - 1
        first, second = x_all[g].astype(F32), x_all[(g + 1) % ROWS].astype(F32)
        put(g, pltpu.roll(jnp.where(lane < HALF, second, first), HALF, 1), 1)

    def make_frames():
        @pl.loop(0, CH)
        def _(c):
            for h in range(2):
                for q in range(4):
                    v = xs[pl.ds(c + (h * (ROWS + 4) + q) * PITCH, ROWS, stride=PITCH), :]
                    frames[c, pl.ds(h * ROWS, ROWS), pl.ds(q * LANES, LANES)] = v.astype(BF16)

    def scalars(i, j):
        return [jnp.clip(scal[n, i * 16 + j], 0, top) for n, top in enumerate((CH - 1, 3, LANES - 1))]

    bands(0, 7)
    for near, far, one in zip(from_two, from_four, from_three):
        near.wait_recv()
        far.start()
        one.start()
    bands(7, PICK)
    for c in (2, 0, 4):
        take(c)
    for cp in from_one:
        cp.wait_recv()
    for c in (1, 3):
        take(c)
    for c in range(4):
        join(c)
    for g in (0, 8):
        levels(g)

    for cp in from_three:
        cp.wait_recv()
    for c in (5, 7):
        take(c)
    for cp in from_four:
        cp.wait_recv()
    take(6)
    for c in range(4, Z):
        join(c)
    for g in (16, 24, 32):
        levels(g)
    make_frames()

    start = (ROWS + 2 * CHUNK - CHUNK * zz) % ROWS
    lane32 = iota((32, LANES), 1)

    def stacks(b):
        @pl.loop(0, min(EACH, PICK - b * EACH))
        def _(ii):
            i = b * EACH + ii
            acc = jnp.zeros((32, LANES), F32)
            for j in range(SLOT):
                c, a, r = scalars(i, j)
                y = nt(frames[c], band[i * SLOT + j])
                y = jnp.concatenate([y[:ROWS], y[ROWS:]], axis=1)
                w = pltpu.roll(y * lev[pl.ds(c, ROWS, stride=PITCH), :], (LANES - r) % LANES, 1)
                rolled[j, pl.ds(0, ROWS), :] = w
                rolled[j, pl.ds(ROWS, 32), :] = w[:32]
                here, after = rolled[j, pl.ds(start + a, 32), :], rolled[j, pl.ds(start + a + 1, 32), :]
                acc += jnp.where(lane32 < LANES - r, here, after)
            outbox[b, pl.ds(ii, 32, stride=EACH), :] = acc

    sends = []
    for b in range(BATCH):
        stacks(b)
        for d in range(1, GROUPS):
            cp = pltpu.make_async_remote_copy(
                src_ref=outbox.at[b, pl.ds(s_peer[d - 1] * 2 * EACH, 2 * EACH)], dst_ref=inbox.at[b, pl.ds(st * 2 * EACH, 2 * EACH)],
                send_sem=a_send.at[b, d - 1], recv_sem=a_recv.at[b, d - 1],
                device_id={"sta": s_peer[d - 1]}, device_id_type=pl.DeviceIdType.MESH)
            cp.start()
            sends.append(cp)
        inbox[b, pl.ds(st * 2 * EACH, 2 * EACH), :] = outbox[b, pl.ds(st * 2 * EACH, 2 * EACH), :]

    hits = [combine_rows(ch_ref[...], h) for h in range(2)]
    total = [0.0, 0.0]
    for b in range(BATCH):
        for cp in sends[b * (GROUPS - 1):(b + 1) * (GROUPS - 1)]:
            cp.wait_recv()
        for h in range(2):
            total[h] += jnp.dot(hits[h][:, b * PART:(b + 1) * PART], inbox[b],
                                precision=lax.Precision.HIGHEST, preferred_element_type=F32)
    for h in range(2):
        o_ref[:, pl.ds(h * LANES, LANES)] = total[h]
    for cp in from_two + from_one + from_four + from_three + sends:
        cp.wait_send()


def shards(waveform, templates, channel, moveout):
    vm = pl.BlockSpec(memory_space=pltpu.VMEM)
    sem = pltpu.SemaphoreType.DMA
    templates = templates.transpose(1, 0, 2)
    return pl.pallas_call(
        kernel,
        out_shape=jax.ShapeDtypeStruct((templates.shape[1], 2 * LANES), F32),
        in_specs=[pl.BlockSpec(memory_space=pl.ANY)] * 4,
        out_specs=vm,
        scratch_shapes=[
            pltpu.VMEM(waveform.shape, BF16),
            pltpu.VMEM(channel.shape, I32),
            pltpu.VMEM(moveout.shape, I32),
            pltpu.VMEM((CHP, 2 * LANES), F32),
            pltpu.VMEM((Y, 2 * CHP, LANES), BF16),
            pltpu.VMEM((ROWS, CHP, LANES), BF16),
            pltpu.VMEM(templates.shape, BF16),
            pltpu.VMEM((8, 256), I32),
            pltpu.SMEM((8, 256), I32),
            pltpu.VMEM((16 * PICK, WIDE), F32),
            pltpu.VMEM((PICK * SLOT, HALF, WIDE), BF16),
            pltpu.VMEM((2 * (ROWS + 4) * PITCH + CHP, LANES), F32),
            pltpu.VMEM(((ROWS + 4) * CHP, LANES), BF16),
            pltpu.VMEM((CH, 2 * ROWS, WIDE), BF16),
            pltpu.VMEM((ROWS * PITCH + CHP, LANES), F32),
            pltpu.VMEM((SLOT, ROWS + 32, LANES), F32),
            pltpu.VMEM((BATCH, PART + 8, LANES), F32),
            pltpu.VMEM((BATCH, PART, LANES), F32),
            sem((Y - 1,)), sem((Y - 1,)), sem((8,)), sem((8,)),
            sem((BATCH, GROUPS - 1)), sem((BATCH, GROUPS - 1)), sem((4,)), sem(()),
        ],
        compiler_params=pltpu.CompilerParams(
            vmem_limit_bytes=56 << 20, collective_id=0, has_side_effects=True
        ),
    )(waveform, templates, channel, moveout)


def solution(mesh):
    placed = (P("sta", "tmpl"), P("tmpl", None, None), P("tmpl", None), P("tmpl", None))
    return jax.shard_map(
        shards, mesh=mesh, in_specs=placed, out_specs=P("tmpl", "sta"), check_vma=False
    )
```

```python
import math

import jax
import jax.numpy as jnp
from jax import lax
from jax.experimental import pallas as pl
from jax.experimental.pallas import tpu as pltpu
from jax.sharding import PartitionSpec as P

F32, BF16, I32 = jnp.float32, jnp.bfloat16, jnp.int32
TAPS = 400
LANES = 128
HALF = 64
WIDE = 512
CH, CHP = 75, 80
LOW, HIGH = 64, 16
PITCH = 84
ROWS = 40
PICK, SLOT = 10, 15
Z, Y, CHUNK = 8, 4, 5
GROUPS = 16
BATCH, EACH = 3, 4
PART = GROUPS * 2 * EACH


def nt(a, b):
    return lax.dot_general(a, b, (((1,), (1,)), ((), ())), preferred_element_type=F32)


def nn(a, b):
    return jnp.dot(a, b, preferred_element_type=F32)


def iota(shape, d):
    return lax.broadcasted_iota(I32, shape, d)


def ones_where(cond):
    return jnp.where(cond, 1.0, 0.0).astype(BF16)


def pair_lists(first, chan, move):
    n, s = chan.shape
    inside = (chan >= first) & (chan < first + CH)
    loc = ones_where(inside)
    slot_rank = nn(loc, ones_where(iota((s, s), 0) < iota((s, s), 1)))
    count = nt(jnp.ones((16, s), BF16), loc)
    rank = nn(ones_where(count > 0.5), ones_where(iota((n, n), 0) < iota((n, n), 1))).astype(I32)
    sel = ones_where((rank == iota((16, n), 0)) & (count > 0.5))

    def keep(v):
        return nn(sel, jnp.where(inside, v, 0).astype(F32).astype(BF16))

    cols = (keep(chan - first), keep(move // LANES), keep(move % LANES), keep(iota((n, s), 0)))
    lsel = nn(sel, loc)
    rsel = nn(sel, slot_rank.astype(BF16)).astype(I32)
    eq = (rsel[:, None, :] == iota((16, 16, s), 1)) & (lsel[:, None, :] > 0.5)
    eq3 = jnp.where(eq, 1.0, 0.0)
    eq = eq3.reshape(256, s).astype(BF16)
    diag = iota((16, 256), 0) == iota((16, 256), 1) // 16
    rows = []
    for v in cols:
        rows.append(jnp.sum(jnp.where(diag, nt(v.astype(BF16), eq), 0.0), axis=0, keepdims=True))
    place = jnp.sum(eq3 * (iota((16, 16, s), 2).astype(F32) * n + cols[3][:, None, :] + 1.0), axis=2, keepdims=True)
    return jnp.concatenate(rows + rows, axis=0).astype(I32), place.reshape(256, 1) - 1.0


def combine_rows(chan, half):
    n = chan.shape[0]
    grp = chan // CH
    low = jnp.min(grp, axis=1, keepdims=True)
    high = jnp.max(grp, axis=1, keepdims=True)
    lane = iota((n, BATCH * PART), 1)
    batch, group, part, row = lane // PART, lane % PART // (2 * EACH), lane % (2 * EACH) // EACH, lane % EACH
    here = (group == low) | (group == high)
    rank = nn(ones_where(iota((n, n), 1) < iota((n, n), 0)), ones_where(here)).astype(I32)
    hit = here & (part == half) & (rank == batch * EACH + row)
    return jnp.where(hit, 1.0, 0.0)


def kernel(w_hbm, t_hbm, ch_hbm, mv_hbm, o_ref,
           w_ref, ch_ref, mv_ref, wide, ybuf, zbuf, x_low, x_high, t_ref, scal_v, scal, units, band, xs, sqs, frames, lev, rolled, outbox, inbox,
           y_send, y_recv, b_send, b_recv, c_send, c_recv, z_send, z_recv, a_send, a_recv, in_sem, s_sem):
    tm, st = lax.axis_index("tmpl"), lax.axis_index("sta")
    zz, yy = tm // Y, tm % Y
    z_peer = {d: (tm + (Z + d) * Y) % (Z * Y) for d in (4, 3, -3, 2, -2, 1, -1)}
    y_peer = [zz * Y + (yy + d) % Y for d in range(1, Y)]
    s_peer = [(st + d) % GROUPS for d in range(1, GROUPS)]

    barrier = pltpu.get_barrier_semaphore()
    for p in y_peer + list(z_peer.values()):
        pl.semaphore_signal(barrier, inc=1, device_id={"tmpl": p}, device_id_type=pl.DeviceIdType.MESH)
    for p in s_peer:
        pl.semaphore_signal(barrier, inc=1, device_id={"sta": p}, device_id_type=pl.DeviceIdType.MESH)

    copies = [pltpu.make_async_copy(src, dst, in_sem.at[n]) for n, (src, dst) in enumerate(
        ((w_hbm, w_ref), (ch_hbm, ch_ref), (mv_hbm, mv_ref), (t_hbm, t_ref)))]
    for cp in copies:
        cp.start()
    outbox[...] = jnp.zeros_like(outbox)

    wide[...] = jnp.zeros_like(wide)
    copies[0].wait()
    wide[pl.ds(0, CH), pl.ds(0, 160)] = w_ref[...].astype(F32)
    own = pltpu.roll(wide[...], 32 * yy, 1)
    one, two = own[:, :LANES].astype(BF16), own[:, LANES:].astype(BF16)
    ybuf[yy] = jnp.concatenate([one[:LOW], two[:LOW]], axis=0)
    zbuf[yy, 2] = jnp.concatenate([one[LOW:], two[LOW:]], axis=0)

    pl.semaphore_wait(barrier, Y - 1 + Z - 1 + GROUPS - 1)

    y_copies = []
    for d in range(1, Y):
        cp = pltpu.make_async_remote_copy(
            src_ref=ybuf.at[yy], dst_ref=ybuf.at[yy], send_sem=y_send.at[d - 1], recv_sem=y_recv.at[d - 1],
            device_id={"tmpl": y_peer[d - 1]}, device_id_type=pl.DeviceIdType.MESH)
        cp.start()
        y_copies.append(cp)

    b_copies = []
    for n, d in enumerate(z_peer):
        cp = pltpu.make_async_remote_copy(
            src_ref=zbuf.at[yy, 2], dst_ref=zbuf.at[yy, (2 - d) % Z], send_sem=b_send.at[n], recv_sem=b_recv.at[n],
            device_id={"tmpl": z_peer[d]}, device_id_type=pl.DeviceIdType.MESH)
        cp.start()
        b_copies.append(cp)

    copies[1].wait()
    copies[2].wait()
    sc, place = pair_lists(st * CH, ch_ref[...], mv_ref[...])
    scal_v[...] = sc
    s_copy = pltpu.make_async_copy(scal_v, scal, s_sem)
    s_copy.start()

    for cp in y_copies:
        cp.wait()

    def blocks(parts, rows):
        parts = [v.astype(F32) for v in parts]
        whole = [parts[0][:rows]] + [parts[n][:rows] + parts[n - 1][rows:] for n in range(1, Y)] + [parts[Y - 1][rows:]]
        return [v.astype(BF16) for v in whole]

    for n, v in enumerate(blocks([ybuf[y] for y in range(Y)], LOW)):
        x_low[2 * CHUNK + n] = v

    def pass_on(n, chunk, d, first=0, count=CHUNK):
        there = (chunk - d) % Z
        return pltpu.make_async_remote_copy(
            src_ref=x_low.at[pl.ds(chunk % Z * CHUNK + first, count)],
            dst_ref=x_low.at[pl.ds(there * CHUNK + first, count)],
            send_sem=z_send.at[n], recv_sem=z_recv.at[n],
            device_id={"tmpl": z_peer[d]}, device_id_type=pl.DeviceIdType.MESH)

    from_two = [pass_on(0, 2, 2), pass_on(1, 2, -2)]
    from_one = [pass_on(2, 2, 1), pass_on(3, 2, -1)]
    from_four = [pass_on(4, 0, 2, 0, 3), pass_on(5, 4, -2, 3, 2)]
    from_three = [pass_on(6, 0, 1), pass_on(7, 4, -1)]
    for cp in from_two + from_one:
        cp.start()

    c_copies = []
    for cp in b_copies:
        cp.wait_recv()
    for d in range(1, Y):
        cp = pltpu.make_async_remote_copy(
            src_ref=zbuf.at[yy], dst_ref=zbuf.at[yy], send_sem=c_send.at[d - 1], recv_sem=c_recv.at[d - 1],
            device_id={"tmpl": y_peer[d - 1]}, device_id_type=pl.DeviceIdType.MESH)
        cp.start()
        c_copies.append(cp)

    copies[3].wait()
    s_copy.wait()

    slots, count = t_ref.shape[:2]
    rows = t_ref[...].reshape(slots * count, TAPS)
    pick = nn(ones_where(place[:16 * PICK].astype(I32) == iota((16 * PICK, slots * count), 1)), rows)
    unit = pick / jnp.sqrt(jnp.sum(pick * pick, axis=1, keepdims=True) / TAPS + 1e-5)
    unit = unit.astype(BF16).astype(F32)
    units[...] = jnp.concatenate([unit, jnp.zeros((16 * PICK, WIDE - TAPS), F32)], axis=1)

    def bands(lo, hi):
        @pl.loop(lo, hi)
        def _(i):
            unit = units[pl.ds(pl.multiple_of(i * 16, 16), 16), :]
            for j in range(SLOT):
                row = jnp.broadcast_to(unit[j:j + 1, :], (HALF, WIDE))
                band[i * SLOT + j] = pltpu.roll(row, 0, 1, stride=1, stride_axis=0).astype(BF16)

    lane = iota((CHP, LANES), 1)

    def put(g, row, odd):
        xs[pl.ds((g + odd * (ROWS + 4)) * PITCH, CHP), :] = row

    def block(g):
        return jnp.concatenate([x_low[g].astype(F32), x_high[g].astype(F32)], axis=0)

    def take(c):
        rows = [block(c * CHUNK + n) for n in range(CHUNK)]
        for n in range(CHUNK):
            again = (0, ROWS) if c == 0 and n < 4 else (0,)
            later = pltpu.roll(jnp.where(lane < HALF, rows[n + 1], rows[n]), HALF, 1) if n < CHUNK - 1 else None
            square = (rows[n] * rows[n]).astype(BF16)
            for more in again:
                g = c * CHUNK + n + more
                put(g, rows[n], 0)
                if later is not None:
                    put(g, later, 1)
                sqs[pl.ds(g * CHP, CHP), :] = square

    e, d = iota((5 * LANES, LANES), 0), iota((5 * LANES, LANES), 1)
    window = ones_where((e >= d) & (e < d + TAPS))
    factor = 1.0 / math.sqrt(TAPS * 2 * SLOT)
    many = 8

    def levels(g):
        s = 0.0
        for q in range(5):
            s += nn(sqs[pl.ds((g + q) * CHP, many * CHP), :], window[q * LANES:(q + 1) * LANES])
        s = lax.rsqrt(s / TAPS + 1e-5) * factor
        for n in range(many):
            lev[pl.ds((g + n) * PITCH, CHP), :] = s[n * CHP:(n + 1) * CHP]

    def join(c):
        g = c * CHUNK + CHUNK - 1
        first, second = block(g), block((g + 1) % ROWS)
        put(g, pltpu.roll(jnp.where(lane < HALF, second, first), HALF, 1), 1)

    def make_frames():
        @pl.loop(0, CH)
        def _(c):
            for h in range(2):
                for q in range(4):
                    v = xs[pl.ds(c + (h * (ROWS + 4) + q) * PITCH, ROWS, stride=PITCH), :]
                    frames[c, pl.ds(h * ROWS, ROWS), pl.ds(q * LANES, LANES)] = v.astype(BF16)

    def scalars(i, j):
        return [jnp.clip(scal[n, i * 16 + j], 0, top) for n, top in enumerate((CH - 1, 3, LANES - 1))]

    bands(0, 7)
    for near, far, one in zip(from_two, from_four, from_three):
        near.wait_recv()
        one.start()
        far.start()
    bands(7, PICK)
    for cp in c_copies:
        cp.wait_recv()
    for c in range(Z):
        for n, v in enumerate(blocks([zbuf[y, c] for y in range(Y)], HIGH)):
            x_high[c * CHUNK + n] = v
    for c in (2, 0, 4):
        take(c)
    for cp in from_one:
        cp.wait_recv()
    for c in (1, 3):
        take(c)
    for c in range(4):
        join(c)
    for g in (0, 8):
        levels(g)

    for cp in from_three:
        cp.wait_recv()
    for c in (5, 7):
        take(c)
    for cp in from_four:
        cp.wait_recv()
    take(6)
    for c in range(4, Z):
        join(c)
    for g in (16, 24, 32):
        levels(g)
    make_frames()

    start = (ROWS + 2 * CHUNK - CHUNK * zz) % ROWS
    lane32 = iota((32, LANES), 1)

    def stacks(b):
        @pl.loop(0, min(EACH, PICK - b * EACH))
        def _(ii):
            i = b * EACH + ii
            acc = jnp.zeros((32, LANES), F32)
            for j in range(SLOT):
                c, a, r = scalars(i, j)
                y = nt(frames[c], band[i * SLOT + j])
                y = jnp.concatenate([y[:ROWS], y[ROWS:]], axis=1)
                w = pltpu.roll(y * lev[pl.ds(c, ROWS, stride=PITCH), :], (LANES - r) % LANES, 1)
                rolled[j, pl.ds(0, ROWS), :] = w
                rolled[j, pl.ds(ROWS, 32), :] = w[:32]
                here, after = rolled[j, pl.ds(start + a, 32), :], rolled[j, pl.ds(start + a + 1, 32), :]
                acc += jnp.where(lane32 < LANES - r, here, after)
            outbox[b, pl.ds(ii, 32, stride=EACH), :] = acc

    sends = []
    for b in range(BATCH):
        stacks(b)
        for d in range(1, GROUPS):
            cp = pltpu.make_async_remote_copy(
                src_ref=outbox.at[b, pl.ds(s_peer[d - 1] * 2 * EACH, 2 * EACH)], dst_ref=inbox.at[b, pl.ds(st * 2 * EACH, 2 * EACH)],
                send_sem=a_send.at[b, d - 1], recv_sem=a_recv.at[b, d - 1],
                device_id={"sta": s_peer[d - 1]}, device_id_type=pl.DeviceIdType.MESH)
            cp.start()
            sends.append(cp)
        inbox[b, pl.ds(st * 2 * EACH, 2 * EACH), :] = outbox[b, pl.ds(st * 2 * EACH, 2 * EACH), :]

    hits = [combine_rows(ch_ref[...], h) for h in range(2)]
    total = [0.0, 0.0]
    for b in range(BATCH):
        for cp in sends[b * (GROUPS - 1):(b + 1) * (GROUPS - 1)]:
            cp.wait_recv()
        for h in range(2):
            total[h] += jnp.dot(hits[h][:, b * PART:(b + 1) * PART], inbox[b],
                                precision=lax.Precision.HIGHEST, preferred_element_type=F32)
    for h in range(2):
        o_ref[:, pl.ds(h * LANES, LANES)] = total[h]
    for cp in b_copies + c_copies + from_two + from_one + from_four + from_three + sends:
        cp.wait_send()


def shards(waveform, templates, channel, moveout):
    vm = pl.BlockSpec(memory_space=pltpu.VMEM)
    sem = pltpu.SemaphoreType.DMA
    templates = templates.transpose(1, 0, 2)
    return pl.pallas_call(
        kernel,
        out_shape=jax.ShapeDtypeStruct((templates.shape[1], 2 * LANES), F32),
        in_specs=[pl.BlockSpec(memory_space=pl.ANY)] * 4,
        out_specs=vm,
        scratch_shapes=[
            pltpu.VMEM(waveform.shape, BF16),
            pltpu.VMEM(channel.shape, I32),
            pltpu.VMEM(moveout.shape, I32),
            pltpu.VMEM((CHP, 2 * LANES), F32),
            pltpu.VMEM((Y, 2 * LOW, LANES), BF16),
            pltpu.VMEM((Y, Z, 2 * HIGH, LANES), BF16),
            pltpu.VMEM((ROWS, LOW, LANES), BF16),
            pltpu.VMEM((ROWS, HIGH, LANES), BF16),
            pltpu.VMEM(templates.shape, BF16),
            pltpu.VMEM((8, 256), I32),
            pltpu.SMEM((8, 256), I32),
            pltpu.VMEM((16 * PICK, WIDE), F32),
            pltpu.VMEM((PICK * SLOT, HALF, WIDE), BF16),
            pltpu.VMEM((2 * (ROWS + 4) * PITCH + CHP, LANES), F32),
            pltpu.VMEM(((ROWS + 4) * CHP, LANES), BF16),
            pltpu.VMEM((CH, 2 * ROWS, WIDE), BF16),
            pltpu.VMEM((ROWS * PITCH + CHP, LANES), F32),
            pltpu.VMEM((SLOT, ROWS + 32, LANES), F32),
            pltpu.VMEM((BATCH, PART + 8, LANES), F32),
            pltpu.VMEM((BATCH, PART, LANES), F32),
            sem((Y - 1,)), sem((Y - 1,)), sem((Z - 1,)), sem((Z - 1,)), sem((Y - 1,)), sem((Y - 1,)), sem((8,)), sem((8,)),
            sem((BATCH, GROUPS - 1)), sem((BATCH, GROUPS - 1)), sem((4,)), sem(()),
        ],
        compiler_params=pltpu.CompilerParams(
            vmem_limit_bytes=56 << 20, collective_id=0, has_side_effects=True
        ),
    )(waveform, templates, channel, moveout)


def solution(mesh):
    placed = (P("sta", "tmpl"), P("tmpl", None, None), P("tmpl", None), P("tmpl", None))
    return jax.shard_map(
        shards, mesh=mesh, in_specs=placed, out_specs=P("tmpl", "sta"), check_vma=False
    )
```

```python
import math

import jax
import jax.numpy as jnp
from jax import lax
from jax.experimental import pallas as pl
from jax.experimental.pallas import tpu as pltpu
from jax.sharding import PartitionSpec as P

F32, BF16, I32 = jnp.float32, jnp.bfloat16, jnp.int32
TAPS = 400
LANES = 128
HALF = 64
WIDE = 512
CH, CHP = 75, 80
LOW, HIGH = 64, 16
PITCH = 84
ROWS = 40
EARLY = 16
PICK, SLOT = 10, 15
Z, Y, CHUNK = 8, 4, 5
GROUPS = 16
BATCH, EACH = 3, 4
PART = GROUPS * 2 * EACH


def nt(a, b):
    return lax.dot_general(a, b, (((1,), (1,)), ((), ())), preferred_element_type=F32)


def nn(a, b):
    return jnp.dot(a, b, preferred_element_type=F32)


def iota(shape, d):
    return lax.broadcasted_iota(I32, shape, d)


def ones_where(cond):
    return jnp.where(cond, 1.0, 0.0).astype(BF16)


def pair_lists(first, chan, move):
    n, s = chan.shape
    inside = (chan >= first) & (chan < first + CH)
    loc = ones_where(inside)
    slot_rank = nn(loc, ones_where(iota((s, s), 0) < iota((s, s), 1)))
    count = nt(jnp.ones((16, s), BF16), loc)
    rank = nn(ones_where(count > 0.5), ones_where(iota((n, n), 0) < iota((n, n), 1))).astype(I32)
    sel = ones_where((rank == iota((16, n), 0)) & (count > 0.5))

    def keep(v):
        return nn(sel, jnp.where(inside, v, 0).astype(F32).astype(BF16))

    cols = (keep(chan - first), keep(move // LANES), keep(move % LANES), keep(iota((n, s), 0)))
    lsel = nn(sel, loc)
    rsel = nn(sel, slot_rank.astype(BF16)).astype(I32)
    eq = (rsel[:, None, :] == iota((16, 16, s), 1)) & (lsel[:, None, :] > 0.5)
    eq3 = jnp.where(eq, 1.0, 0.0)
    eq = eq3.reshape(256, s).astype(BF16)
    diag = iota((16, 256), 0) == iota((16, 256), 1) // 16
    rows = []
    for v in cols:
        rows.append(jnp.sum(jnp.where(diag, nt(v.astype(BF16), eq), 0.0), axis=0, keepdims=True))
    place = jnp.sum(eq3 * (iota((16, 16, s), 2).astype(F32) * n + cols[3][:, None, :] + 1.0), axis=2, keepdims=True)
    return jnp.concatenate(rows + rows, axis=0).astype(I32), place.reshape(256, 1) - 1.0


def combine_rows(chan, half):
    n = chan.shape[0]
    grp = chan // CH
    low = jnp.min(grp, axis=1, keepdims=True)
    high = jnp.max(grp, axis=1, keepdims=True)
    lane = iota((n, BATCH * PART), 1)
    batch, group, part, row = lane // PART, lane % PART // (2 * EACH), lane % (2 * EACH) // EACH, lane % EACH
    here = (group == low) | (group == high)
    rank = nn(ones_where(iota((n, n), 1) < iota((n, n), 0)), ones_where(here)).astype(I32)
    hit = here & (part == half) & (rank == batch * EACH + row)
    return jnp.where(hit, 1.0, 0.0)


def kernel(w_hbm, t_hbm, ch_hbm, mv_hbm, o_ref,
           w_ref, ch_ref, mv_ref, wide, ybuf, zbuf, x_low, x_high, t_ref, scal_v, scal, units, band, xs, sqs, frames, lev, rolled, outbox, inbox,
           y_send, y_recv, b_send, b_recv, c_send, c_recv, z_send, z_recv, a_send, a_recv, in_sem, s_sem):
    tm, st = lax.axis_index("tmpl"), lax.axis_index("sta")
    zz, yy = tm // Y, tm % Y
    z_peer = {d: (tm + (Z + d) * Y) % (Z * Y) for d in (4, 3, -3, 2, -2, 1, -1)}
    y_peer = [zz * Y + (yy + d) % Y for d in range(1, Y)]
    s_peer = [(st + d) % GROUPS for d in range(1, GROUPS)]

    barrier = pltpu.get_barrier_semaphore()
    for p in y_peer + list(z_peer.values()):
        pl.semaphore_signal(barrier, inc=1, device_id={"tmpl": p}, device_id_type=pl.DeviceIdType.MESH)
    for p in s_peer:
        pl.semaphore_signal(barrier, inc=1, device_id={"sta": p}, device_id_type=pl.DeviceIdType.MESH)

    copies = [pltpu.make_async_copy(src, dst, in_sem.at[n]) for n, (src, dst) in enumerate(
        ((w_hbm, w_ref), (ch_hbm, ch_ref), (mv_hbm, mv_ref), (t_hbm, t_ref)))]
    for cp in copies:
        cp.start()
    outbox[...] = jnp.zeros_like(outbox)

    wide[...] = jnp.zeros_like(wide)
    copies[0].wait()
    wide[pl.ds(0, CH), pl.ds(0, 160)] = w_ref[...].astype(F32)
    own = pltpu.roll(wide[...], 32 * yy, 1)
    one, two = own[:, :LANES].astype(BF16), own[:, LANES:].astype(BF16)
    ybuf[yy] = jnp.concatenate([one[:LOW], two[:LOW]], axis=0)
    zbuf[yy, 2] = jnp.concatenate([one[LOW:], two[LOW:]], axis=0)

    pl.semaphore_wait(barrier, Y - 1 + Z - 1 + GROUPS - 1)

    y_copies = []
    for d in range(1, Y):
        cp = pltpu.make_async_remote_copy(
            src_ref=ybuf.at[yy], dst_ref=ybuf.at[yy], send_sem=y_send.at[d - 1], recv_sem=y_recv.at[d - 1],
            device_id={"tmpl": y_peer[d - 1]}, device_id_type=pl.DeviceIdType.MESH)
        cp.start()
        y_copies.append(cp)

    b_copies = []
    for n, d in enumerate(z_peer):
        cp = pltpu.make_async_remote_copy(
            src_ref=zbuf.at[yy, 2], dst_ref=zbuf.at[yy, (2 - d) % Z], send_sem=b_send.at[n], recv_sem=b_recv.at[n],
            device_id={"tmpl": z_peer[d]}, device_id_type=pl.DeviceIdType.MESH)
        cp.start()
        b_copies.append(cp)

    copies[1].wait()
    copies[2].wait()
    sc, place = pair_lists(st * CH, ch_ref[...], mv_ref[...])
    scal_v[...] = sc
    s_copy = pltpu.make_async_copy(scal_v, scal, s_sem)
    s_copy.start()

    for cp in y_copies:
        cp.wait()

    def blocks(parts, rows):
        parts = [v.astype(F32) for v in parts]
        whole = [parts[0][:rows]] + [parts[n][:rows] + parts[n - 1][rows:] for n in range(1, Y)] + [parts[Y - 1][rows:]]
        return [v.astype(BF16) for v in whole]

    for n, v in enumerate(blocks([ybuf[y] for y in range(Y)], LOW)):
        x_low[2 * CHUNK + n] = v

    def pass_on(n, chunk, d, first=0, count=CHUNK):
        there = (chunk - d) % Z
        return pltpu.make_async_remote_copy(
            src_ref=x_low.at[pl.ds(chunk % Z * CHUNK + first, count)],
            dst_ref=x_low.at[pl.ds(there * CHUNK + first, count)],
            send_sem=z_send.at[n], recv_sem=z_recv.at[n],
            device_id={"tmpl": z_peer[d]}, device_id_type=pl.DeviceIdType.MESH)

    from_two = [pass_on(0, 2, 2), pass_on(1, 2, -2)]
    from_one = [pass_on(2, 2, 1), pass_on(3, 2, -1)]
    from_four = [pass_on(4, 0, 2, 0, 3), pass_on(5, 4, -2, 3, 2)]
    from_three = [pass_on(6, 0, 1), pass_on(7, 4, -1)]
    for cp in from_two + from_one:
        cp.start()

    c_copies = []
    for cp in b_copies:
        cp.wait_recv()
    for d in range(1, Y):
        cp = pltpu.make_async_remote_copy(
            src_ref=zbuf.at[yy], dst_ref=zbuf.at[yy], send_sem=c_send.at[d - 1], recv_sem=c_recv.at[d - 1],
            device_id={"tmpl": y_peer[d - 1]}, device_id_type=pl.DeviceIdType.MESH)
        cp.start()
        c_copies.append(cp)

    copies[3].wait()
    s_copy.wait()

    slots, count = t_ref.shape[:2]
    rows = t_ref[...].reshape(slots * count, TAPS)
    pick = nn(ones_where(place[:16 * PICK].astype(I32) == iota((16 * PICK, slots * count), 1)), rows)
    unit = pick / jnp.sqrt(jnp.sum(pick * pick, axis=1, keepdims=True) / TAPS + 1e-5)
    unit = unit.astype(BF16).astype(F32)
    units[...] = jnp.concatenate([unit, jnp.zeros((16 * PICK, WIDE - TAPS), F32)], axis=1)

    def bands(lo, hi):
        @pl.loop(lo, hi)
        def _(i):
            unit = units[pl.ds(pl.multiple_of(i * 16, 16), 16), :]
            for j in range(SLOT):
                row = jnp.broadcast_to(unit[j:j + 1, :], (HALF, WIDE))
                band[i * SLOT + j] = pltpu.roll(row, 0, 1, stride=1, stride_axis=0).astype(BF16)

    lane = iota((CHP, LANES), 1)

    def put(g, row, odd):
        xs[pl.ds((g + odd * (ROWS + 4)) * PITCH, CHP), :] = row

    def block(g):
        return jnp.concatenate([x_low[g].astype(F32), x_high[g].astype(F32)], axis=0)

    def take(c):
        rows = [block(c * CHUNK + n) for n in range(CHUNK)]
        for n in range(CHUNK):
            again = (0, ROWS) if c == 0 and n < 4 else (0,)
            later = pltpu.roll(jnp.where(lane < HALF, rows[n + 1], rows[n]), HALF, 1) if n < CHUNK - 1 else None
            square = (rows[n] * rows[n]).astype(BF16)
            for more in again:
                g = c * CHUNK + n + more
                put(g, rows[n], 0)
                if later is not None:
                    put(g, later, 1)
                sqs[pl.ds(g * CHP, CHP), :] = square

    e, d = iota((5 * LANES, LANES), 0), iota((5 * LANES, LANES), 1)
    window = ones_where((e >= d) & (e < d + TAPS))
    factor = 1.0 / math.sqrt(TAPS * 2 * SLOT)
    many = 8

    def levels(g):
        s = 0.0
        for q in range(5):
            s += nn(sqs[pl.ds((g + q) * CHP, many * CHP), :], window[q * LANES:(q + 1) * LANES])
        s = lax.rsqrt(s / TAPS + 1e-5) * factor
        for n in range(many):
            lev[pl.ds((g + n) * PITCH, CHP), :] = s[n * CHP:(n + 1) * CHP]

    def join(c):
        g = c * CHUNK + CHUNK - 1
        first, second = block(g), block((g + 1) % ROWS)
        put(g, pltpu.roll(jnp.where(lane < HALF, second, first), HALF, 1), 1)

    def make_frames(first, count):
        @pl.loop(0, CH // 5)
        def _(c5):
            for u in range(5):
                c = c5 * 5 + u
                for h in range(2):
                    for q in range(4):
                        v = xs[pl.ds(c + (h * (ROWS + 4) + q + first) * PITCH, count, stride=PITCH), :]
                        frames[c, pl.ds(2 * first + h * count, count), pl.ds(q * LANES, LANES)] = v.astype(BF16)

    def scalars(i, j):
        return [jnp.clip(scal[n, i * 16 + j], 0, top) for n, top in enumerate((CH - 1, 3, LANES - 1))]

    bands(0, 7)
    for near, far, one in zip(from_two, from_four, from_three):
        near.wait_recv()
        one.start()
        far.start()
    bands(7, PICK)
    for cp in c_copies:
        cp.wait_recv()
    for c in range(Z):
        for n, v in enumerate(blocks([zbuf[y, c] for y in range(Y)], HIGH)):
            x_high[c * CHUNK + n] = v
    for c in (2, 0, 4):
        take(c)
    for cp in from_one:
        cp.wait_recv()
    for c in (1, 3):
        take(c)
    for c in range(4):
        join(c)
    for g in (0, 8):
        levels(g)
    make_frames(0, EARLY)

    for cp in from_three:
        cp.wait_recv()
    for c in (5, 7):
        take(c)
    for cp in from_four:
        cp.wait_recv()
    take(6)
    for c in range(4, Z):
        join(c)
    for g in (16, 24, 32):
        levels(g)
    make_frames(EARLY, ROWS - EARLY)

    start = (ROWS + 2 * CHUNK - CHUNK * zz) % ROWS
    lane32 = iota((32, LANES), 1)

    def stacks(b):
        @pl.loop(0, min(EACH, PICK - b * EACH) // 2)
        def _(some):
            for u in range(2):
                i = b * EACH + some * 2 + u
                acc = jnp.zeros((32, LANES), F32)
                for j in range(SLOT):
                    c, a, r = scalars(i, j)
                    y = nt(frames[c], band[i * SLOT + j])
                    even = jnp.concatenate([y[:EARLY], y[2 * EARLY:ROWS + EARLY]], axis=0)
                    odd = jnp.concatenate([y[EARLY:2 * EARLY], y[ROWS + EARLY:]], axis=0)
                    y = jnp.concatenate([even, odd], axis=1)
                    w = pltpu.roll(y * lev[pl.ds(c, ROWS, stride=PITCH), :], (LANES - r) % LANES, 1)
                    n = u * SLOT + j
                    rolled[n, pl.ds(0, ROWS), :] = w
                    rolled[n, pl.ds(ROWS, 32), :] = w[:32]
                    here, after = rolled[n, pl.ds(start + a, 32), :], rolled[n, pl.ds(start + a + 1, 32), :]
                    acc += jnp.where(lane32 < LANES - r, here, after)
                outbox[b, pl.ds(some * 2 + u, 32, stride=EACH), :] = acc

    sends = []
    for b in range(BATCH):
        stacks(b)
        for d in range(1, GROUPS):
            cp = pltpu.make_async_remote_copy(
                src_ref=outbox.at[b, pl.ds(s_peer[d - 1] * 2 * EACH, 2 * EACH)], dst_ref=inbox.at[b, pl.ds(st * 2 * EACH, 2 * EACH)],
                send_sem=a_send.at[b, d - 1], recv_sem=a_recv.at[b, d - 1],
                device_id={"sta": s_peer[d - 1]}, device_id_type=pl.DeviceIdType.MESH)
            cp.start()
            sends.append(cp)
        inbox[b, pl.ds(st * 2 * EACH, 2 * EACH), :] = outbox[b, pl.ds(st * 2 * EACH, 2 * EACH), :]

    hits = [combine_rows(ch_ref[...], h) for h in range(2)]
    total = [0.0, 0.0]
    for b in range(BATCH):
        for cp in sends[b * (GROUPS - 1):(b + 1) * (GROUPS - 1)]:
            cp.wait_recv()
        for h in range(2):
            total[h] += jnp.dot(hits[h][:, b * PART:(b + 1) * PART], inbox[b],
                                precision=lax.Precision.HIGHEST, preferred_element_type=F32)
    for h in range(2):
        o_ref[:, pl.ds(h * LANES, LANES)] = total[h]
    for cp in b_copies + c_copies + from_two + from_one + from_four + from_three + sends:
        cp.wait_send()


def shards(waveform, templates, channel, moveout):
    vm = pl.BlockSpec(memory_space=pltpu.VMEM)
    sem = pltpu.SemaphoreType.DMA
    templates = templates.transpose(1, 0, 2)
    return pl.pallas_call(
        kernel,
        out_shape=jax.ShapeDtypeStruct((templates.shape[1], 2 * LANES), F32),
        in_specs=[pl.BlockSpec(memory_space=pl.ANY)] * 4,
        out_specs=vm,
        scratch_shapes=[
            pltpu.VMEM(waveform.shape, BF16),
            pltpu.VMEM(channel.shape, I32),
            pltpu.VMEM(moveout.shape, I32),
            pltpu.VMEM((CHP, 2 * LANES), F32),
            pltpu.VMEM((Y, 2 * LOW, LANES), BF16),
            pltpu.VMEM((Y, Z, 2 * HIGH, LANES), BF16),
            pltpu.VMEM((ROWS, LOW, LANES), BF16),
            pltpu.VMEM((ROWS, HIGH, LANES), BF16),
            pltpu.VMEM(templates.shape, BF16),
            pltpu.VMEM((8, 256), I32),
            pltpu.SMEM((8, 256), I32),
            pltpu.VMEM((16 * PICK, WIDE), F32),
            pltpu.VMEM((PICK * SLOT, HALF, WIDE), BF16),
            pltpu.VMEM((2 * (ROWS + 4) * PITCH + CHP, LANES), F32),
            pltpu.VMEM(((ROWS + 4) * CHP, LANES), BF16),
            pltpu.VMEM((CH, 2 * ROWS, WIDE), BF16),
            pltpu.VMEM((ROWS * PITCH + CHP, LANES), F32),
            pltpu.VMEM((2 * SLOT, ROWS + 32, LANES), F32),
            pltpu.VMEM((BATCH, PART + 8, LANES), F32),
            pltpu.VMEM((BATCH, PART, LANES), F32),
            sem((Y - 1,)), sem((Y - 1,)), sem((Z - 1,)), sem((Z - 1,)), sem((Y - 1,)), sem((Y - 1,)), sem((8,)), sem((8,)),
            sem((BATCH, GROUPS - 1)), sem((BATCH, GROUPS - 1)), sem((4,)), sem(()),
        ],
        compiler_params=pltpu.CompilerParams(
            vmem_limit_bytes=56 << 20, collective_id=0, has_side_effects=True
        ),
    )(waveform, templates, channel, moveout)


def solution(mesh):
    placed = (P("sta", "tmpl"), P("tmpl", None, None), P("tmpl", None), P("tmpl", None))
    return jax.shard_map(
        shards, mesh=mesh, in_specs=placed, out_specs=P("tmpl", "sta"), check_vma=False
    )
```

```python
import math

import jax
import jax.numpy as jnp
from jax import lax
from jax.experimental import pallas as pl
from jax.experimental.pallas import tpu as pltpu
from jax.sharding import PartitionSpec as P

F32, BF16, I32 = jnp.float32, jnp.bfloat16, jnp.int32
TAPS = 400
LANES = 128
HALF = 64
WIDE = 512
CH, CHP = 75, 80
LOW, HIGH = 64, 16
PITCH = 84
ROWS = 40
EARLY = 16
PICK, SLOT = 10, 15
Z, Y, CHUNK = 8, 4, 5
GROUPS = 16
BATCH, EACH = 3, 4
PART = GROUPS * 2 * EACH


def nt(a, b):
    return lax.dot_general(a, b, (((1,), (1,)), ((), ())), preferred_element_type=F32)


def nn(a, b):
    return jnp.dot(a, b, preferred_element_type=F32)


def iota(shape, d):
    return lax.broadcasted_iota(I32, shape, d)


def ones_where(cond):
    return jnp.where(cond, 1.0, 0.0).astype(BF16)


def pair_lists(first, chan, move):
    n, s = chan.shape
    inside = (chan >= first) & (chan < first + CH)
    loc = ones_where(inside)
    slot_rank = nn(loc, ones_where(iota((s, s), 0) < iota((s, s), 1)))
    count = nt(jnp.ones((16, s), BF16), loc)
    rank = nn(ones_where(count > 0.5), ones_where(iota((n, n), 0) < iota((n, n), 1))).astype(I32)
    sel = ones_where((rank == iota((16, n), 0)) & (count > 0.5))

    def keep(v):
        return nn(sel, jnp.where(inside, v, 0).astype(F32).astype(BF16))

    cols = (keep(chan - first), keep(move // LANES), keep(move % LANES), keep(iota((n, s), 0)))
    lsel = nn(sel, loc)
    rsel = nn(sel, slot_rank.astype(BF16)).astype(I32)
    eq = (rsel[:, None, :] == iota((16, 16, s), 1)) & (lsel[:, None, :] > 0.5)
    eq3 = jnp.where(eq, 1.0, 0.0)
    eq = eq3.reshape(256, s).astype(BF16)
    diag = iota((16, 256), 0) == iota((16, 256), 1) // 16
    rows = []
    for v in cols:
        rows.append(jnp.sum(jnp.where(diag, nt(v.astype(BF16), eq), 0.0), axis=0, keepdims=True))
    place = jnp.sum(eq3 * (iota((16, 16, s), 2).astype(F32) * n + cols[3][:, None, :] + 1.0), axis=2, keepdims=True)
    return jnp.concatenate(rows + rows, axis=0).astype(I32), place.reshape(256, 1) - 1.0


def combine_rows(chan, half):
    n = chan.shape[0]
    grp = chan // CH
    low = jnp.min(grp, axis=1, keepdims=True)
    high = jnp.max(grp, axis=1, keepdims=True)
    lane = iota((n, BATCH * PART), 1)
    batch, group, part, row = lane // PART, lane % PART // (2 * EACH), lane % (2 * EACH) // EACH, lane % EACH
    here = (group == low) | (group == high)
    rank = nn(ones_where(iota((n, n), 1) < iota((n, n), 0)), ones_where(here)).astype(I32)
    hit = here & (part == half) & (rank == batch * EACH + row)
    return jnp.where(hit, 1.0, 0.0)


def kernel(w_hbm, t_hbm, ch_hbm, mv_hbm, o_ref,
           w_ref, ch_ref, mv_ref, wide, ybuf, zbuf, x_low, x_high, t_ref, scal_v, scal, units, band, xs, sqs, frames, lev, rolled, outbox, inbox,
           y_send, y_recv, b_send, b_recv, c_send, c_recv, z_send, z_recv, a_send, a_recv, in_sem, s_sem):
    tm, st = lax.axis_index("tmpl"), lax.axis_index("sta")
    zz, yy = tm // Y, tm % Y
    z_peer = {d: (tm + (Z + d) * Y) % (Z * Y) for d in (4, 3, -3, 2, -2, 1, -1)}
    y_peer = [zz * Y + (yy + d) % Y for d in range(1, Y)]
    s_peer = [(st + d) % GROUPS for d in range(1, GROUPS)]

    barrier = pltpu.get_barrier_semaphore()
    for p in y_peer + list(z_peer.values()):
        pl.semaphore_signal(barrier, inc=1, device_id={"tmpl": p}, device_id_type=pl.DeviceIdType.MESH)
    for p in s_peer:
        pl.semaphore_signal(barrier, inc=1, device_id={"sta": p}, device_id_type=pl.DeviceIdType.MESH)

    copies = [pltpu.make_async_copy(src, dst, in_sem.at[n]) for n, (src, dst) in enumerate(
        ((w_hbm, w_ref), (ch_hbm, ch_ref), (mv_hbm, mv_ref), (t_hbm, t_ref)))]
    for cp in copies:
        cp.start()
    outbox[...] = jnp.zeros_like(outbox)

    wide[...] = jnp.zeros_like(wide)
    copies[0].wait()
    wide[pl.ds(0, CH), pl.ds(0, 160)] = w_ref[...].astype(F32)
    own = pltpu.roll(wide[...], 32 * yy, 1)
    one, two = own[:, :LANES].astype(BF16), own[:, LANES:].astype(BF16)
    ybuf[yy] = jnp.concatenate([one[:LOW], two[:LOW]], axis=0)
    zbuf[yy, 2] = jnp.concatenate([one[LOW:], two[LOW:]], axis=0)

    pl.semaphore_wait(barrier, Y - 1 + Z - 1 + GROUPS - 1)

    y_copies = []
    for d in range(1, Y):
        cp = pltpu.make_async_remote_copy(
            src_ref=ybuf.at[yy], dst_ref=ybuf.at[yy], send_sem=y_send.at[d - 1], recv_sem=y_recv.at[d - 1],
            device_id={"tmpl": y_peer[d - 1]}, device_id_type=pl.DeviceIdType.MESH)
        cp.start()
        y_copies.append(cp)

    b_copies = []
    for n, d in enumerate(z_peer):
        cp = pltpu.make_async_remote_copy(
            src_ref=zbuf.at[yy, 2], dst_ref=zbuf.at[yy, (2 - d) % Z], send_sem=b_send.at[n], recv_sem=b_recv.at[n],
            device_id={"tmpl": z_peer[d]}, device_id_type=pl.DeviceIdType.MESH)
        cp.start()
        b_copies.append(cp)

    copies[1].wait()
    copies[2].wait()
    sc, place = pair_lists(st * CH, ch_ref[...], mv_ref[...])
    scal_v[...] = sc
    s_copy = pltpu.make_async_copy(scal_v, scal, s_sem)
    s_copy.start()

    for cp in y_copies:
        cp.wait()

    def blocks(parts, rows):
        parts = [v.astype(F32) for v in parts]
        whole = [parts[0][:rows]] + [parts[n][:rows] + parts[n - 1][rows:] for n in range(1, Y)] + [parts[Y - 1][rows:]]
        return [v.astype(BF16) for v in whole]

    for n, v in enumerate(blocks([ybuf[y] for y in range(Y)], LOW)):
        x_low[2 * CHUNK + n] = v

    def pass_on(n, chunk, d, first=0, count=CHUNK):
        there = (chunk - d) % Z
        return pltpu.make_async_remote_copy(
            src_ref=x_low.at[pl.ds(chunk % Z * CHUNK + first, count)],
            dst_ref=x_low.at[pl.ds(there * CHUNK + first, count)],
            send_sem=z_send.at[n], recv_sem=z_recv.at[n],
            device_id={"tmpl": z_peer[d]}, device_id_type=pl.DeviceIdType.MESH)

    from_two = [pass_on(0, 2, 2), pass_on(1, 2, -2)]
    from_one = [pass_on(2, 2, 1), pass_on(3, 2, -1)]
    from_four = [pass_on(4, 0, 2, 0, 3), pass_on(5, 4, -2, 3, 2)]
    from_three = [pass_on(6, 0, 1), pass_on(7, 4, -1)]
    for cp in from_two + from_one:
        cp.start()

    c_copies = []
    for cp in b_copies:
        cp.wait_recv()
    for d in range(1, Y):
        cp = pltpu.make_async_remote_copy(
            src_ref=zbuf.at[yy], dst_ref=zbuf.at[yy], send_sem=c_send.at[d - 1], recv_sem=c_recv.at[d - 1],
            device_id={"tmpl": y_peer[d - 1]}, device_id_type=pl.DeviceIdType.MESH)
        cp.start()
        c_copies.append(cp)

    copies[3].wait()
    s_copy.wait()

    slots, count = t_ref.shape[:2]
    rows = t_ref[...].reshape(slots * count, TAPS)
    pick = nn(ones_where(place[:16 * PICK].astype(I32) == iota((16 * PICK, slots * count), 1)), rows)
    unit = pick / jnp.sqrt(jnp.sum(pick * pick, axis=1, keepdims=True) / TAPS + 1e-5)
    unit = unit.astype(BF16).astype(F32)
    units[...] = jnp.concatenate([unit, jnp.zeros((16 * PICK, WIDE - TAPS), F32)], axis=1)

    def bands(lo, hi):
        @pl.loop(lo, hi)
        def _(i):
            unit = units[pl.ds(pl.multiple_of(i * 16, 16), 16), :]
            for j in range(SLOT):
                row = jnp.broadcast_to(unit[j:j + 1, :], (HALF, WIDE))
                band[i * SLOT + j] = pltpu.roll(row, 0, 1, stride=1, stride_axis=0).astype(BF16)

    lane = iota((CHP, LANES), 1)

    def put(g, row, odd):
        xs[pl.ds((g + odd * (ROWS + 4)) * PITCH, CHP), :] = row

    def block(g):
        return jnp.concatenate([x_low[g].astype(F32), x_high[g].astype(F32)], axis=0)

    def take(c):
        rows = [block(c * CHUNK + n) for n in range(CHUNK)]
        for n in range(CHUNK):
            again = (0, ROWS) if c == 0 and n < 4 else (0,)
            later = pltpu.roll(jnp.where(lane < HALF, rows[n + 1], rows[n]), HALF, 1) if n < CHUNK - 1 else None
            square = (rows[n] * rows[n]).astype(BF16)
            for more in again:
                g = c * CHUNK + n + more
                put(g, rows[n], 0)
                if later is not None:
                    put(g, later, 1)
                sqs[pl.ds(g * CHP, CHP), :] = square

    e, d = iota((5 * LANES, LANES), 0), iota((5 * LANES, LANES), 1)
    window = ones_where((e >= d) & (e < d + TAPS))
    factor = 1.0 / math.sqrt(TAPS * 2 * SLOT)
    many = 8

    def levels(g):
        s = 0.0
        for q in range(5):
            s += nn(sqs[pl.ds((g + q) * CHP, many * CHP), :], window[q * LANES:(q + 1) * LANES])
        s = lax.rsqrt(s / TAPS + 1e-5) * factor
        for n in range(many):
            lev[pl.ds((g + n) * PITCH, CHP), :] = s[n * CHP:(n + 1) * CHP]

    def join(c):
        g = c * CHUNK + CHUNK - 1
        first, second = block(g), block((g + 1) % ROWS)
        put(g, pltpu.roll(jnp.where(lane < HALF, second, first), HALF, 1), 1)

    def make_frames(first, count):
        @pl.loop(0, CH // 5)
        def _(c5):
            for u in range(5):
                c = c5 * 5 + u
                for h in range(2):
                    for q in range(4):
                        v = xs[pl.ds(c + (h * (ROWS + 4) + q + first) * PITCH, count, stride=PITCH), :]
                        frames[c, pl.ds(2 * first + h * count, count), pl.ds(q * LANES, LANES)] = v.astype(BF16)

    def scalars(i, j):
        return [jnp.clip(scal[n, i * 16 + j], 0, top) for n, top in enumerate((CH - 1, 3, LANES - 1))]

    bands(0, 7)
    for near, far, one in zip(from_two, from_four, from_three):
        near.wait_recv()
        one.start()
        far.start()
    bands(7, PICK)
    for cp in c_copies:
        cp.wait_recv()
    for c in range(Z):
        for n, v in enumerate(blocks([zbuf[y, c] for y in range(Y)], HIGH)):
            x_high[c * CHUNK + n] = v
    for c in (2, 0, 4):
        take(c)
    for cp in from_one:
        cp.wait_recv()
    for c in (1, 3):
        take(c)
    for c in range(4):
        join(c)
    for g in (0, 8):
        levels(g)
    make_frames(0, EARLY)

    for cp in from_three:
        cp.wait_recv()
    for c in (5, 7):
        take(c)
    for cp in from_four:
        cp.wait_recv()
    take(6)
    for c in range(4, Z):
        join(c)
    for g in (16, 24, 32):
        levels(g)
    make_frames(EARLY, ROWS - EARLY)

    start = (ROWS + 2 * CHUNK - CHUNK * zz) % ROWS
    lane32 = iota((32, LANES), 1)

    def stacks(b):
        size = min(EACH, PICK - b * EACH)

        @pl.loop(0, 1)
        def _(some):
            for u in range(size):
                i = b * EACH + some * size + u
                acc = jnp.zeros((32, LANES), F32)
                for j in range(SLOT):
                    c, a, r = scalars(i, j)
                    y = nt(frames[c], band[i * SLOT + j])
                    even = jnp.concatenate([y[:EARLY], y[2 * EARLY:ROWS + EARLY]], axis=0)
                    odd = jnp.concatenate([y[EARLY:2 * EARLY], y[ROWS + EARLY:]], axis=0)
                    y = jnp.concatenate([even, odd], axis=1)
                    w = pltpu.roll(y * lev[pl.ds(c, ROWS, stride=PITCH), :], (LANES - r) % LANES, 1)
                    n = u * SLOT + j
                    rolled[n, pl.ds(0, ROWS), :] = w
                    rolled[n, pl.ds(ROWS, 32), :] = w[:32]
                    here, after = rolled[n, pl.ds(start + a, 32), :], rolled[n, pl.ds(start + a + 1, 32), :]
                    acc += jnp.where(lane32 < LANES - r, here, after)
                outbox[b, pl.ds(some * size + u, 32, stride=EACH), :] = acc

    sends = []
    for b in range(BATCH):
        stacks(b)
        for d in range(1, GROUPS):
            cp = pltpu.make_async_remote_copy(
                src_ref=outbox.at[b, pl.ds(s_peer[d - 1] * 2 * EACH, 2 * EACH)], dst_ref=inbox.at[b, pl.ds(st * 2 * EACH, 2 * EACH)],
                send_sem=a_send.at[b, d - 1], recv_sem=a_recv.at[b, d - 1],
                device_id={"sta": s_peer[d - 1]}, device_id_type=pl.DeviceIdType.MESH)
            cp.start()
            sends.append(cp)
        inbox[b, pl.ds(st * 2 * EACH, 2 * EACH), :] = outbox[b, pl.ds(st * 2 * EACH, 2 * EACH), :]

    hits = [combine_rows(ch_ref[...], h) for h in range(2)]
    total = [0.0, 0.0]
    for b in range(BATCH):
        for cp in sends[b * (GROUPS - 1):(b + 1) * (GROUPS - 1)]:
            cp.wait_recv()
        for h in range(2):
            total[h] += jnp.dot(hits[h][:, b * PART:(b + 1) * PART], inbox[b],
                                precision=lax.Precision.HIGHEST, preferred_element_type=F32)
    for h in range(2):
        o_ref[:, pl.ds(h * LANES, LANES)] = total[h]
    for cp in b_copies + c_copies + from_two + from_one + from_four + from_three + sends:
        cp.wait_send()


def shards(waveform, templates, channel, moveout):
    vm = pl.BlockSpec(memory_space=pltpu.VMEM)
    sem = pltpu.SemaphoreType.DMA
    templates = templates.transpose(1, 0, 2)
    return pl.pallas_call(
        kernel,
        out_shape=jax.ShapeDtypeStruct((templates.shape[1], 2 * LANES), F32),
        in_specs=[pl.BlockSpec(memory_space=pl.ANY)] * 4,
        out_specs=vm,
        scratch_shapes=[
            pltpu.VMEM(waveform.shape, BF16),
            pltpu.VMEM(channel.shape, I32),
            pltpu.VMEM(moveout.shape, I32),
            pltpu.VMEM((CHP, 2 * LANES), F32),
            pltpu.VMEM((Y, 2 * LOW, LANES), BF16),
            pltpu.VMEM((Y, Z, 2 * HIGH, LANES), BF16),
            pltpu.VMEM((ROWS, LOW, LANES), BF16),
            pltpu.VMEM((ROWS, HIGH, LANES), BF16),
            pltpu.VMEM(templates.shape, BF16),
            pltpu.VMEM((8, 256), I32),
            pltpu.SMEM((8, 256), I32),
            pltpu.VMEM((16 * PICK, WIDE), F32),
            pltpu.VMEM((PICK * SLOT, HALF, WIDE), BF16),
            pltpu.VMEM((2 * (ROWS + 4) * PITCH + CHP, LANES), F32),
            pltpu.VMEM(((ROWS + 4) * CHP, LANES), BF16),
            pltpu.VMEM((CH, 2 * ROWS, WIDE), BF16),
            pltpu.VMEM((ROWS * PITCH + CHP, LANES), F32),
            pltpu.VMEM((4 * SLOT, ROWS + 32, LANES), F32),
            pltpu.VMEM((BATCH, PART + 8, LANES), F32),
            pltpu.VMEM((BATCH, PART, LANES), F32),
            sem((Y - 1,)), sem((Y - 1,)), sem((Z - 1,)), sem((Z - 1,)), sem((Y - 1,)), sem((Y - 1,)), sem((8,)), sem((8,)),
            sem((BATCH, GROUPS - 1)), sem((BATCH, GROUPS - 1)), sem((4,)), sem(()),
        ],
        compiler_params=pltpu.CompilerParams(
            vmem_limit_bytes=56 << 20, collective_id=0, has_side_effects=True
        ),
    )(waveform, templates, channel, moveout)


def solution(mesh):
    placed = (P("sta", "tmpl"), P("tmpl", None, None), P("tmpl", None), P("tmpl", None))
    return jax.shard_map(
        shards, mesh=mesh, in_specs=placed, out_specs=P("tmpl", "sta"), check_vma=False
    )
```
